512 devices in a mesh: section: 8 (over y_hi, x), dp: 64 (over y_lo, z, core).
Axes of the slice: x: 4, y: 8 (y_hi: 2, y_lo: 4; y = y_hi * 4 + y_lo), z: 8, core: 2. Of those that a mesh axis runs over, the one named last changes fastest.
Arguments:
- embeds: bfloat16 [12288, 3584], P('dp'), may hold values from -16 to 16
- cotangent: bfloat16 [12288, 3584], P('dp'), may hold values from -1 to 1
- adapter_a: bfloat16 [8, 7168, 128], P('section', 'dp'), may hold values from -0.0625 to 0.0625
- adapter_b: bfloat16 [8, 128, 3584], P('section', None, 'dp'), may hold values from -0.5 to 0.5
- norm_gains: float32 [2, 7168], replicated, may hold values from 0.5 to 1.5
Outputs:
- grad_a: float32 [8, 7168, 128], P('section', 'dp')
- grad_b: float32 [8, 128, 3584], P('section')
- grad_gain: float32 [2, 7168], P(None, 'dp')
- grad_embed: bfloat16 [12288, 3584], P('dp', 'section')
The draws below stay inside these ranges and needn't reach their ends.
All inputs are finite; a program needn't handle non-finite values.
Results may differ from the reference program's by a relative error of at most 0.023.
Values may be sent and summed in bfloat16 or wider, within the bound.
A program may use at most 64 MiB of HBM per device.

```python
import math
import jax
import jax.numpy as jnp
from jax import lax

D = 3584
R = 128
CAT = 7168
TOKENS = 12288
SECTIONS = 8


def draw_embeds(key, part):
    row_key, col_key, base_key = jax.random.split(key, 3)
    row_scale = jnp.exp(jax.random.uniform(row_key, (TOKENS, 1), jnp.float32, math.log(0.3), math.log(3.0)))
    col_scale = jnp.exp(jax.random.uniform(col_key, (1, D), jnp.float32, math.log(0.3), math.log(3.0)))
    base_draw = jax.random.normal(base_key, (TOKENS, D), jnp.float32)
    return jnp.clip(base_draw * row_scale * col_scale, -16.0, 16.0).astype(jnp.bfloat16)


def strengthened(result, rng, source, target, shards_of, factor):
    owner, partner = [(jnp.arange(result.shape[dim]) // (result.shape[dim] // shards_of)).reshape([-1 if axis == dim else 1 for axis in range(result.ndim)]) for dim in (source, target)]
    chosen = jax.random.permutation(rng, shards_of)[partner]
    strong = (owner == chosen) | (owner == (partner + shards_of // 2) % shards_of)
    return jnp.where(strong, factor * result, result)


def shard_levels(stream_key, extent, cuts, smallest, largest):
    gain = 1.0
    for dim, blocks in cuts:
        draws = jax.random.uniform(jax.random.fold_in(jax.random.fold_in(stream_key, 6), dim), (blocks,), jnp.float32, smallest / len(cuts), largest / len(cuts))
        gain = gain * jnp.repeat(jnp.exp(draws), extent[dim] // blocks).reshape((-1,) + (1,) * (len(extent) - 1 - dim))
    return gain


def noise(own_key, dims, scale, limit, pieces=(), kind=jnp.bfloat16):
    result = scale * jax.random.normal(own_key, dims, jnp.float32)
    if pieces:
        result = result * shard_levels(own_key, dims, pieces, -0.22, 0.18)
    return jnp.clip(result, -limit, limit).astype(kind)


def heavy_noise(own_key, dims, spread, reach, cuts, heavy, held_as=jnp.bfloat16):
    result = spread * jax.random.normal(own_key, dims, jnp.float32)
    if cuts:
        result = result * shard_levels(own_key, dims, cuts, -0.22, 0.18)
    return jnp.clip(strengthened(result, jax.random.fold_in(own_key, 3), *heavy), -reach, reach).astype(held_as)


def setup_inputs(seed: int = 0) -> dict:
    splits = jax.random.split(jax.random.key(seed), 6)
    embeds = draw_embeds(jax.random.fold_in(splits[5], 71), 0)
    cotangent = heavy_noise(splits[1], (TOKENS, D), 0.125, 1.0, ((0, 64),), (0, 1, 64, 4.0))
    adapter_a = noise(splits[2], (SECTIONS, CAT, R), CAT ** -0.5, 0.0625, ((0, 8), (1, 64)))
    adapter_b = noise(splits[3], (SECTIONS, R, D), R ** -0.5, 0.5, ((0, 8), (2, 64)))
    norm_gains = jnp.clip(1.0 + 0.1 * jax.random.normal(splits[4], (2, CAT), jnp.float32), 0.5, 1.5)
    return dict(embeds=embeds, cotangent=cotangent, adapter_a=adapter_a, adapter_b=adapter_b, norm_gains=norm_gains)


epsilon = 1e-05

def normalize(hidden, embeds, gain_row):
    joined = jnp.concatenate([hidden.astype(jnp.float32), embeds.astype(jnp.float32)], axis=1)
    inv_rms = lax.rsqrt(lax.optimization_barrier(jnp.mean(joined * joined, axis=1, keepdims=True)) + epsilon)
    normed = joined * inv_rms
    lowered = (normed * gain_row[None, :]).astype(jnp.bfloat16)
    return (normed, inv_rms, lowered)

def reference(embeds, cotangent, adapter_a, adapter_b, norm_gains):
    hidden = embeds
    inputs = []
    for section in range(SECTIONS):
        normed, inv_rms, lowered = normalize(hidden, embeds, norm_gains[section % 2])
        reduced = jnp.dot(lowered, adapter_a[section], preferred_element_type=jnp.float32).astype(jnp.bfloat16)
        inputs.append(hidden)
        hidden = (hidden.astype(jnp.float32) + jnp.dot(reduced, adapter_b[section], preferred_element_type=jnp.float32)).astype(jnp.bfloat16)
    back = cotangent
    grads_a = []
    grads_b = []
    gain_total = jnp.zeros((2, CAT), jnp.float32)
    embed_total = jnp.zeros((TOKENS, D), jnp.float32)
    for section in reversed(range(SECTIONS)):
        gain_row = norm_gains[section % 2]
        normed, inv_rms, lowered = normalize(inputs[section], embeds, gain_row)
        reduced = jnp.dot(lowered, adapter_a[section], preferred_element_type=jnp.float32).astype(jnp.bfloat16)
        up_grad = jnp.dot(back, adapter_b[section].T, preferred_element_type=jnp.float32).astype(jnp.bfloat16)
        grads_b.append(jnp.dot(reduced.T, back, preferred_element_type=jnp.float32))
        grad_lowered = jnp.dot(up_grad, adapter_a[section].T, preferred_element_type=jnp.float32)
        grads_a.append(jnp.dot(lowered.T, up_grad, preferred_element_type=jnp.float32))
        gain_part = lax.optimization_barrier(jnp.sum(grad_lowered * normed, axis=0)).astype(jnp.bfloat16)
        gain_part = lax.optimization_barrier(gain_part)
        scaled = grad_lowered * gain_row[None, :]
        grad_joined = inv_rms * (scaled - normed * lax.optimization_barrier(jnp.mean(scaled * normed, axis=1, keepdims=True)))
        back = (back.astype(jnp.float32) + grad_joined[:, :D]).astype(jnp.bfloat16)
        embed_tail = grad_joined[:, D:]
        if section == 0:
            embed_tail = embed_tail + back.astype(jnp.float32)
        embed_part = lax.optimization_barrier(embed_tail.astype(jnp.bfloat16))
        embed_total = embed_total + embed_part.astype(jnp.float32)
        gain_total = gain_total.at[section % 2].add(gain_part.astype(jnp.float32))
    grad_a = jnp.stack(grads_a[::-1])
    grad_b = jnp.stack(grads_b[::-1])
    return (grad_a, grad_b, gain_total, embed_total.astype(jnp.bfloat16))
```

```python
import functools

import jax
import jax.numpy as jnp
from jax import lax
from jax.experimental import pallas as pl
from jax.experimental.pallas import tpu as pltpu
from jax.sharding import PartitionSpec as P

EPS = 1e-05
CALLS = 8
DP = (4, 8, 2)
SEC = (2, 4)
BF = jnp.bfloat16
F32 = jnp.float32
MESH = pl.DeviceIdType.MESH
NT = (((1,), (1,)), ((), ()))


def start_barrier(peers):
    sem = pltpu.get_barrier_semaphore()
    for peer in peers:
        pl.semaphore_signal(sem, inc=1, device_id=peer, device_id_type=MESH)
    pl.semaphore_wait(sem, len(peers))


def remote(src, dst, send, recv, peer):
    return pltpu.make_async_remote_copy(
        src_ref=src, dst_ref=dst, send_sem=send, recv_sem=recv, device_id=peer, device_id_type=MESH
    )


def dp_place(dims):
    _, zs, cs = dims
    me = lax.axis_index("dp")
    return me // (zs * cs), lax.rem(me // cs, zs), lax.rem(me, cs)


def dp_peer(dims, y, z, c):
    _, zs, cs = dims
    return {"dp": (y * zs + z) * cs + c}


def hops(zs, stream, ys):
    long_way, short_way = zs // 2, zs - 1 - zs // 2
    return (long_way, short_way) if stream < ys // 2 else (short_way, long_way)


def gather_dp_kernel(dims, x_ref, out_ref, local_sem, ysend, yrecv, zsend, zrecv, csend, crecv):
    ys, zs, cs = dims
    y0, z0, c0 = dp_place(dims)
    right, left = lax.rem(z0 + 1, zs), lax.rem(z0 + zs - 1, zs)
    sides = (right, left)
    peers = [dp_peer(dims, lax.rem(y0 + j, ys), z0, c0) for j in range(1, ys)]
    peers += [dp_peer(dims, y0, right, c0), dp_peer(dims, y0, left, c0)]
    sibling = dp_peer(dims, y0, z0, 1 - c0)
    start_barrier(peers + [sibling])

    own = pltpu.make_async_copy(x_ref, out_ref.at[y0, z0, c0], local_sem)
    own.start()
    sent = []
    for j in range(1, ys):
        copy = remote(x_ref, out_ref.at[y0, z0, c0], ysend.at[j], yrecv.at[j], peers[j - 1])
        copy.start()
        sent.append(copy)
    own.wait()
    rows = [lax.rem(y0 + ys - j, ys) for j in range(ys)]

    def origin(side, k):
        return lax.rem(z0 + zs - k, zs) if side == 0 else lax.rem(z0 + k, zs)

    def share(j, z, index):
        block = out_ref.at[rows[j], z, c0]
        copy = remote(block, block, csend.at[j, index], crecv.at[j, index], sibling)
        copy.start()
        sent.append(copy)

    def relay(j, side, k):
        block = out_ref.at[rows[j], origin(side, k), c0]
        copy = remote(
            block, block, zsend.at[side, j, k], zrecv.at[side, j, k], dp_peer(dims, y0, sides[side], c0)
        )
        copy.start()
        sent.append(copy)

    for j in range(ys):
        if j:
            block = out_ref.at[rows[j], z0, c0]
            remote(block, block, ysend.at[j], yrecv.at[j], peers[j - 1]).wait_recv()
        for side in range(2):
            if hops(zs, j, ys)[side]:
                relay(j, side, 0)
        share(j, z0, 0)
    for k in range(1, zs // 2 + 1):
        for j in range(ys):
            for side in range(2):
                count = hops(zs, j, ys)[side]
                if k <= count:
                    block = out_ref.at[rows[j], origin(side, k), c0]
                    remote(
                        block,
                        block,
                        zsend.at[side, j, k - 1],
                        zrecv.at[side, j, k - 1],
                        dp_peer(dims, y0, sides[side], c0),
                    ).wait_recv()
                    if k < count:
                        relay(j, side, k)
                    share(j, origin(side, k), zs - k if side == 0 else k)
    for j in range(ys):
        for index in range(zs):
            block = out_ref.at[rows[j], lax.rem(z0 + index, zs), 1 - c0]
            remote(block, block, csend.at[j, index], crecv.at[j, index], sibling).wait_recv()
    for copy in sent:
        copy.wait_send()


def gather_dp(x, collective_id, dims=DP):
    ys, zs, cs = dims
    dma = pltpu.SemaphoreType.DMA
    return pl.pallas_call(
        functools.partial(gather_dp_kernel, dims),
        out_shape=jax.ShapeDtypeStruct(dims + x.shape, x.dtype),
        in_specs=[pl.BlockSpec(memory_space=pl.ANY)],
        out_specs=pl.BlockSpec(memory_space=pl.ANY),
        scratch_shapes=[
            dma,
            dma((ys,)),
            dma((ys,)),
            dma((2, ys, zs // 2)),
            dma((2, ys, zs // 2)),
            dma((ys, zs)),
            dma((ys, zs)),
        ],
        compiler_params=pltpu.CompilerParams(collective_id=collective_id, has_side_effects=True),
    )(x)


def sec_place(secs):
    me = lax.axis_index("section")
    return me // secs[1], lax.rem(me, secs[1])


def gather_sec_kernel(secs, x_ref, out_ref, local_sem, ysend, yrecv, xsend, xrecv):
    width = secs[1]
    y0, x0 = sec_place(secs)
    across = {"section": (1 - y0) * width + x0}
    beside = [{"section": y0 * width + lax.rem(x0 + j, width)} for j in range(1, width)]
    start_barrier([across] + beside)
    own = pltpu.make_async_copy(x_ref, out_ref.at[y0, x0], local_sem)
    own.start()
    sent = [remote(x_ref, out_ref.at[y0, x0], ysend, yrecv, across)]
    sent[0].start()
    for j in range(1, width):
        copy = remote(x_ref, out_ref.at[y0, x0], xsend.at[0, j], xrecv.at[0, j], beside[j - 1])
        copy.start()
        sent.append(copy)
    block = out_ref.at[1 - y0, x0]
    remote(block, block, ysend, yrecv, across).wait_recv()
    for j in range(1, width):
        copy = remote(block, block, xsend.at[1, j], xrecv.at[1, j], beside[j - 1])
        copy.start()
        sent.append(copy)
    for h in range(2):
        for j in range(1, width):
            row = y0 if h == 0 else 1 - y0
            landed = out_ref.at[row, lax.rem(x0 + width - j, width)]
            remote(landed, landed, xsend.at[h, j], xrecv.at[h, j], beside[j - 1]).wait_recv()
    own.wait()
    for copy in sent:
        copy.wait_send()


def gather_sec(x, collective_id, secs=SEC):
    dma = pltpu.SemaphoreType.DMA
    return pl.pallas_call(
        functools.partial(gather_sec_kernel, secs),
        out_shape=jax.ShapeDtypeStruct(secs + x.shape, x.dtype),
        in_specs=[pl.BlockSpec(memory_space=pl.ANY)],
        out_specs=pl.BlockSpec(memory_space=pl.ANY),
        scratch_shapes=[dma, dma, dma, dma((2, secs[1])), dma((2, secs[1]))],
        compiler_params=pltpu.CompilerParams(collective_id=collective_id, has_side_effects=True),
    )(x)


def sum_sec_kernel(count, x_ref, out_ref, landing, send1, recv1, send2, recv2):
    me = lax.axis_index("section")
    peers = [{"section": lax.rem(me + j, count)} for j in range(1, count)]
    start_barrier(peers)
    sent = []
    for j in range(1, count):
        copy = remote(
            x_ref.at[lax.rem(me + j, count)], landing.at[me], send1.at[j], recv1.at[j], peers[j - 1]
        )
        copy.start()
        sent.append(copy)
    total = x_ref[me].astype(F32)
    for j in range(1, count):
        source = lax.rem(me + count - j, count)
        block = landing.at[source]
        remote(block, block, send1.at[j], recv1.at[j], peers[j - 1]).wait_recv()
        total = total + landing[source].astype(F32)
    out_ref[me] = total.astype(out_ref.dtype)
    for j in range(1, count):
        block = out_ref.at[me]
        copy = remote(block, block, send2.at[j], recv2.at[j], peers[j - 1])
        copy.start()
        sent.append(copy)
    for j in range(1, count):
        block = out_ref.at[lax.rem(me + count - j, count)]
        remote(block, block, send2.at[j], recv2.at[j], peers[j - 1]).wait_recv()
    for copy in sent:
        copy.wait_send()


def sum_sec(x, collective_id):
    count = x.shape[0]
    dma = pltpu.SemaphoreType.DMA
    return pl.pallas_call(
        functools.partial(sum_sec_kernel, count),
        out_shape=jax.ShapeDtypeStruct(x.shape, x.dtype),
        in_specs=[pl.BlockSpec(memory_space=pltpu.VMEM)],
        out_specs=pl.BlockSpec(memory_space=pltpu.VMEM),
        scratch_shapes=[pltpu.VMEM(x.shape, x.dtype), dma((count,)), dma((count,)), dma((count,)), dma((count,))],
        compiler_params=pltpu.CompilerParams(collective_id=collective_id, has_side_effects=True),
    )(x)


def scatter_dp_kernel(
    dims, x_ref, out_ref, from_core, moving, landing, rest, from_row, csend, crecv, zsend, zrecv, ysend, yrecv
):
    ys, zs, cs = dims
    y0, z0, c0 = dp_place(dims)
    right, left = lax.rem(z0 + 1, zs), lax.rem(z0 + zs - 1, zs)
    sides = (dp_peer(dims, y0, right, c0), dp_peer(dims, y0, left, c0))
    rows = [dp_peer(dims, lax.rem(y0 + j, ys), z0, c0) for j in range(1, ys)]
    sibling = dp_peer(dims, y0, z0, 1 - c0)
    start_barrier(list(sides) + rows + [sibling])
    sent = []


    order = []
    for reach in range(zs // 2, -1, -1):
        for offset in {reach, (zs - reach) % zs}:
            order.append(offset)
    order = sorted(set(order), key=lambda o: -min(o, zs - o))
    for offset in order:
        z = lax.rem(z0 + offset, zs)
        copy = remote(
            x_ref.at[:, z, 1 - c0], from_core.at[offset], csend.at[offset], crecv.at[offset], sibling
        )
        copy.start()
        sent.append(copy)

    def core_sum(offset, j):
        z = lax.rem(z0 + offset, zs)
        return x_ref[j, z, c0].astype(F32) + from_core[offset, j].astype(F32)

    ready = set()

    def need(offset):
        if offset not in ready:
            ready.add(offset)
            block = from_core.at[offset]
            remote(block, block, csend.at[offset], crecv.at[offset], sibling).wait_recv()

    totals = {}
    for k in range(zs // 2 + 1):
        for j in range(ys):
            for side in range(2):
                count = hops(zs, j, ys)[side]
                step = k - (zs // 2 - count)
                if step < 0 or step > count:
                    continue
                reach = count - step
                offset = reach if side == 0 else (zs - reach) % zs
                if step:
                    block = landing.at[side, j, step - 1]
                    remote(
                        block, block, zsend.at[side, j, step - 1], zrecv.at[side, j, step - 1], sides[side]
                    ).wait_recv()
                    got = landing[side, j, step - 1].astype(F32)
                if reach:
                    need(offset)
                    value = core_sum(offset, j)
                    if step:
                        value = value + got
                    moving[side, j, step] = value.astype(moving.dtype)
                    copy = remote(
                        moving.at[side, j, step],
                        landing.at[side, j, step],
                        zsend.at[side, j, step],
                        zrecv.at[side, j, step],
                        sides[side],
                    )
                    copy.start()
                    sent.append(copy)
                else:
                    if j not in totals:
                        need(0)
                        totals[j] = core_sum(0, j) + got
                    else:
                        rest[j] = (totals[j] + got).astype(rest.dtype)
    own = jnp.zeros(out_ref.shape, F32)
    for i in range(1, ys):
        row = lax.rem(y0 + i, ys)
        copy = remote(rest.at[row], from_row.at[i], ysend.at[i], yrecv.at[i], rows[i - 1])
        copy.start()
        sent.append(copy)
    own = rest[y0].astype(F32)
    for i in range(1, ys):
        block = from_row.at[i]
        remote(block, block, ysend.at[i], yrecv.at[i], rows[i - 1]).wait_recv()
        own = own + from_row[i].astype(F32)
    out_ref[...] = own
    for copy in sent:
        copy.wait_send()


def scatter_dp(x, collective_id, dims=DP):
    ys, zs, cs = dims
    block = x.shape[1:]
    x = x.reshape(dims + block)
    dma = pltpu.SemaphoreType.DMA
    half = zs // 2
    return pl.pallas_call(
        functools.partial(scatter_dp_kernel, dims),
        out_shape=jax.ShapeDtypeStruct(block, F32),
        in_specs=[pl.BlockSpec(memory_space=pltpu.VMEM)],
        out_specs=pl.BlockSpec(memory_space=pltpu.VMEM),
        scratch_shapes=[
            pltpu.VMEM((zs, ys) + block, x.dtype),
            pltpu.VMEM((2, ys, half) + block, x.dtype),
            pltpu.VMEM((2, ys, half) + block, x.dtype),
            pltpu.VMEM((ys,) + block, x.dtype),
            pltpu.VMEM((ys,) + block, x.dtype),
            dma((zs,)),
            dma((zs,)),
            dma((2, ys, half)),
            dma((2, ys, half)),
            dma((ys,)),
            dma((ys,)),
        ],
        compiler_params=pltpu.CompilerParams(
            collective_id=collective_id, has_side_effects=True, vmem_limit_bytes=40 * 2**20
        ),
    )(x)


def dot(a, b):
    return jnp.dot(a, b, preferred_element_type=F32)


def dot_nt(a, b):
    return lax.dot_general(a, b, NT, preferred_element_type=F32)


def solve_kernel(
    proj_ref,
    e2_ref,
    gram_ref,
    et_ref,
    ct_ref,
    a1_ref,
    a2_ref,
    bt_ref,
    out_ref,
    ge_ref,
    r_ref,
    v_ref,
    w_ref,
    hb_ref,
    h_ref,
    acc_ref,
):
    tokens, rank = r_ref.shape[1:]
    cols = et_ref.shape[0]
    scale = 1.0 / (2 * cols * CALLS)

    def gram(t, block):
        return gram_ref[t, :, block].reshape(rank, rank)

    e2 = e2_ref[:, :1]
    h2 = e2
    invs = []
    for s in range(CALLS):
        pre = proj_ref[s, :, :rank].astype(F32)
        hb = proj_ref[s, :, rank : 2 * rank].astype(F32)
        for t in range(s):
            pre = pre + dot(r_ref[t], gram(t, 2 * s))
            hb = hb + dot(r_ref[t], gram(t, 2 * s + 1))
        inv = lax.rsqrt((e2 + h2) * scale + EPS)
        invs.append(inv)
        r = (pre * inv).astype(BF)
        r_ref[s] = r
        rn = dot(r, gram(s, 2 * s + 1))
        h2 = h2 + jnp.sum(r.astype(F32) * (2.0 * hb + rn), axis=1, keepdims=True)
        hb_ref[s] = hb + rn

    lane = lax.broadcasted_iota(jnp.int32, (tokens, rank), 1)
    kap = jnp.zeros((tokens, 1), F32)
    kmat = jnp.zeros((tokens, rank), F32)
    for s in reversed(range(CALLS)):
        u = proj_ref[s, :, 2 * rank :].astype(F32) - kap * hb_ref[s]
        for t in range(s + 1, CALLS):
            u = u + dot_nt(v_ref[t], gram(s, 2 * t)) + dot_nt(w_ref[t], gram(s, 2 * t + 1))
        u = u.astype(BF).astype(F32)
        r = r_ref[s].astype(F32)
        inv = invs[s]
        q = jnp.sum(u * r, axis=1, keepdims=True) * scale
        k = inv * inv * q
        v_ref[s] = (inv * u).astype(BF)
        w_ref[s] = (-kap * r).astype(BF)
        kmat = jnp.where(lane == s, k, kmat)
        kap = kap + k

    unit = (
        lax.broadcasted_iota(jnp.int32, (CALLS, rank), 0) == lax.broadcasted_iota(jnp.int32, (CALLS, rank), 1)
    ).astype(F32)
    krows = lax.dot_general(unit, kmat, NT, precision=lax.Precision.HIGHEST, preferred_element_type=F32)

    quarter, eighth = cols // 4, cols // 8
    filler = jnp.zeros((out_ref.shape[1] - quarter - eighth, rank), F32)
    h_ref[0] = et_ref[...]
    for t in range(CALLS):
        h = h_ref[t]
        top = dot(h, v_ref[t]).astype(BF)
        low = dot(et_ref[...], v_ref[t]).astype(BF)
        for j in range(4):
            out_ref[t * 4 + j, :quarter] = top[j * quarter : (j + 1) * quarter]
            out_ref[CALLS * 4 + t * 4 + j, :quarter] = low[j * quarter : (j + 1) * quarter]
        if t + 1 < CALLS:
            h_ref[t + 1] = (h.astype(F32) + dot_nt(bt_ref[t], r_ref[t])).astype(BF)
    back = ct_ref[...]
    acc_ref[...] = jnp.zeros(acc_ref.shape, F32)
    for t in reversed(range(CALLS)):
        part = dot(back, r_ref[t])
        for j in range(8):
            piece = jnp.concatenate([part[j * eighth : (j + 1) * eighth], filler], axis=0)
            out_ref[t * 8 + j, quarter:] = piece.astype(BF)
        krow = krows[t : t + 1]
        step = dot_nt(a1_ref[t], v_ref[t]) - krow * h_ref[t].astype(F32)
        back = (back.astype(F32) + step).astype(BF)
        acc_ref[...] += dot_nt(a2_ref[t], v_ref[t]) - krow * et_ref[...].astype(F32)
    ge_ref[...] = (acc_ref[...] + back.astype(F32)).astype(BF)


def solve(proj, e2, gram, et, ct, a1, a2, bt):
    cols, tokens = et.shape
    rank = bt.shape[-1]
    vmem = pl.BlockSpec(memory_space=pltpu.VMEM)
    return pl.pallas_call(
        solve_kernel,
        out_shape=[
            jax.ShapeDtypeStruct((64, cols // 4 + 64, rank), BF),
            jax.ShapeDtypeStruct((cols, tokens), BF),
        ],
        in_specs=[vmem] * 8,
        out_specs=[vmem] * 2,
        scratch_shapes=[
            pltpu.VMEM((CALLS, tokens, rank), BF),
            pltpu.VMEM((CALLS, tokens, rank), BF),
            pltpu.VMEM((CALLS, tokens, rank), BF),
            pltpu.VMEM((CALLS, tokens, rank), F32),
            pltpu.VMEM((CALLS, cols, tokens), BF),
            pltpu.VMEM((cols, tokens), F32),
        ],
        compiler_params=pltpu.CompilerParams(vmem_limit_bytes=48 * 2**20),
    )(proj, e2, gram, et, ct, a1, a2, bt)


def route(place):
    return [(s * 64 + d, place(s, d)) for s in range(CALLS) for d in range(64)]


def place_a(t, d):
    return (d % 32) // 4 * 64 + d // 32 * 32 + t * 4 + d % 4


def place_b(t, d):
    return d // 8 * 64 + t * 8 + d % 8


def moved(block, place, back=False):
    pairs = route(place)
    if back:
        pairs = [(b, a) for a, b in pairs]
    return lax.ppermute(block, ("section", "dp"), pairs)


def per_device(embeds, cotangent, adapter_a, adapter_b, norm_gains):
    sec = lax.axis_index("section")
    dp = lax.axis_index("dp")
    width = embeds.shape[1]
    cols = width // CALLS
    a_own = adapter_a[0]
    rank = a_own.shape[1]
    bt_own = adapter_b[0].T
    quarter, eighth = a_own.shape[0], bt_own.shape[0]
    pad = 64 - eighth
    b_pad = jnp.pad(bt_own, ((0, pad), (0, 0)))
    a_moved = moved(a_own, place_a)
    b_moved = moved(b_pad, place_b)
    sheet = gather_dp(jnp.concatenate([a_own, b_pad, a_moved, b_moved], axis=0), 0)
    sheet = sheet.reshape(64, 2 * (quarter + 64), rank)
    half = quarter + 64
    gain = jnp.where(sec % 2 == 0, norm_gains[0], norm_gains[1])
    down = sheet[:, :quarter].reshape(2, width, rank).astype(F32)
    pmat = (down[0] * gain[:width, None] + down[1] * gain[width:, None]).astype(BF)
    up = sheet[:, quarter : quarter + eighth].reshape(width, rank)
    proj = jnp.concatenate([dot(embeds, jnp.concatenate([pmat, up], axis=1)), dot(cotangent, up)], axis=1)
    proj = gather_sec(proj.astype(BF), 1).reshape(CALLS, embeds.shape[0], 3 * rank)

    gcols = lax.dynamic_slice_in_dim(norm_gains.reshape(2, 2, CALLS, cols), sec, 1, 2)[:, :, 0]
    gcalls = jnp.stack([gcols[t % 2] for t in range(CALLS)], axis=1)
    parts = sheet[:, half : half + quarter].reshape(2, CALLS, cols, rank).astype(F32)
    parts = (parts * gcalls[..., None]).astype(BF)
    bt_cols = sheet[:, half + quarter : half + quarter + eighth].reshape(CALLS, cols, rank)
    brows = lax.dynamic_index_in_dim(bt_cols, dp // 8, 0, keepdims=False)
    brows = lax.dynamic_slice_in_dim(brows, (dp % 8) * 16, 16, 1)
    both = jnp.stack([parts[0], bt_cols], axis=1)
    gpart = lax.dot_general(brows, both, (((0,), (2,)), ((), ())), preferred_element_type=F32)
    gpart = gpart.transpose(1, 2, 0, 3).reshape(CALLS, 32, rank).astype(BF)
    gram = sum_sec(gpart, 2).reshape(256, rank)
    gram = gather_dp(gram, 3).reshape(CALLS, 8, 16, 16, rank)

    esq = embeds.astype(F32)
    e2 = jnp.broadcast_to(jnp.sum(esq * esq, axis=1, keepdims=True), (embeds.shape[0], rank))
    et = lax.dynamic_slice_in_dim(embeds, sec * cols, cols, 1).T
    ct = lax.dynamic_slice_in_dim(cotangent, sec * cols, cols, 1).T
    terms, ge = solve(proj, e2, gram, et, ct, parts[0], parts[1], bt_cols)

    own = scatter_dp(terms, 4)
    w = moved(own[:quarter].astype(BF), place_a, True).astype(F32)
    gb = moved(own[quarter:].astype(BF), place_b, True)
    gain_rows = lax.dynamic_slice_in_dim(gain, dp * quarter, quarter, 0)
    grad_a = w * gain_rows[:, None]
    gain_part = jnp.sum(w * a_own.astype(F32), axis=1).astype(BF).astype(F32)
    gain_part = jnp.pad(gain_part[None], ((0, 7), (0, rank - quarter)))
    gains = gather_sec(gain_part, 5).reshape(CALLS // 2, 2, 8, rank)[:, :, 0, :quarter]
    grad_gain = jnp.sum(gains, axis=0)
    grad_b = gather_dp(gb, 6).reshape(64, 64, rank)[:, :eighth].reshape(width, rank)
    return (grad_a[None], grad_b.T.astype(F32)[None], grad_gain, ge.T)


def solution(mesh):
    in_specs = (
        P("dp", None),
        P("dp", None),
        P("section", "dp", None),
        P("section", None, "dp"),
        P(),
    )
    out_specs = (
        P("section", "dp", None),
        P("section", None, None),
        P(None, "dp"),
        P("dp", "section"),
    )
    return jax.shard_map(per_device, mesh=mesh, in_specs=in_specs, out_specs=out_specs, check_vma=False)
```

```python
import functools

import jax
import jax.numpy as jnp
from jax import lax
from jax.experimental import pallas as pl
from jax.experimental.pallas import tpu as pltpu
from jax.sharding import PartitionSpec as P

EPS = 1e-05
CALLS = 8
DP = (4, 8, 2)
SEC = (2, 4)
BF = jnp.bfloat16
F32 = jnp.float32
MESH = pl.DeviceIdType.MESH
NT = (((1,), (1,)), ((), ()))


def start_barrier(peers, swaps=()):
    sem = pltpu.get_barrier_semaphore()
    count = len(peers)
    for peer in peers:
        pl.semaphore_signal(sem, inc=1, device_id=peer, device_id_type=MESH)
    for swap in swaps:
        swap.greet(sem)
        count = count + jnp.where(swap.stays, 0, 1)
    pl.semaphore_wait(sem, count)


def remote(src, dst, send, recv, peer):
    return pltpu.make_async_remote_copy(
        src_ref=src, dst_ref=dst, send_sem=send, recv_sem=recv, device_id=peer, device_id_type=MESH
    )


def hops(zs, stream, ys):
    long_way, short_way = zs // 2, zs - 1 - zs // 2
    return (long_way, short_way) if stream < ys // 2 else (short_way, long_way)


class Ring:
    def __init__(self, dims):
        self.dims = dims
        ys, zs, cs = dims
        me = lax.axis_index("dp")
        self.y, self.z, self.c = me // (zs * cs), lax.rem(me // cs, zs), lax.rem(me, cs)
        self.rows = [self.at(lax.rem(self.y + j, ys), self.z, self.c) for j in range(1, ys)]
        right, left = lax.rem(self.z + 1, zs), lax.rem(self.z + zs - 1, zs)
        self.sides = (self.at(self.y, right, self.c), self.at(self.y, left, self.c))
        self.sibling = self.at(self.y, self.z, 1 - self.c)
        self.peers = self.rows + list(self.sides) + [self.sibling]

    def at(self, y, z, c):
        _, zs, cs = self.dims
        return {"dp": (y * zs + z) * cs + c}


def ring_sems(dims):
    ys, zs, _ = dims
    dma = pltpu.SemaphoreType.DMA
    return [
        dma,
        dma((ys,)),
        dma((ys,)),
        dma((2, ys, zs // 2)),
        dma((2, ys, zs // 2)),
        dma((ys, zs)),
        dma((ys, zs)),
    ]


def spread(ring, src, out_ref, sems, between=None):
    local_sem, ysend, yrecv, zsend, zrecv, csend, crecv = sems
    ys, zs, cs = ring.dims
    y0, z0, c0 = ring.y, ring.z, ring.c
    own = pltpu.make_async_copy(src, out_ref.at[y0, z0, c0], local_sem)
    own.start()
    sent = []
    for j in range(1, ys):
        copy = remote(src, out_ref.at[y0, z0, c0], ysend.at[j], yrecv.at[j], ring.rows[j - 1])
        copy.start()
        sent.append(copy)
    lines = [lax.rem(y0 + ys - j, ys) for j in range(ys)]

    def origin(side, k):
        return lax.rem(z0 + zs - k, zs) if side == 0 else lax.rem(z0 + k, zs)

    def share(j, z, index):
        block = out_ref.at[lines[j], z, c0]
        copy = remote(
            block if index or j else src, block, csend.at[j, index], crecv.at[j, index], ring.sibling
        )
        copy.start()
        sent.append(copy)

    def relay(j, side, k):
        block = out_ref.at[lines[j], origin(side, k), c0]
        copy = remote(
            block if k or j else src, block, zsend.at[side, j, k], zrecv.at[side, j, k], ring.sides[side]
        )
        copy.start()
        sent.append(copy)

    for j in range(ys):
        if j:
            block = out_ref.at[lines[j], z0, c0]
            remote(block, block, ysend.at[j], yrecv.at[j], ring.rows[j - 1]).wait_recv()
        for side in range(2):
            if hops(zs, j, ys)[side]:
                relay(j, side, 0)
        share(j, z0, 0)
    if between is not None:
        between()
    for k in range(1, zs // 2 + 1):
        for j in range(ys):
            for side in range(2):
                count = hops(zs, j, ys)[side]
                if k <= count:
                    block = out_ref.at[lines[j], origin(side, k), c0]
                    remote(
                        block, block, zsend.at[side, j, k - 1], zrecv.at[side, j, k - 1], ring.sides[side]
                    ).wait_recv()
                    if k < count:
                        relay(j, side, k)
                    share(j, origin(side, k), zs - k if side == 0 else k)
    for j in range(ys):
        for index in range(zs):
            block = out_ref.at[lines[j], lax.rem(z0 + index, zs), 1 - c0]
            remote(block, block, csend.at[j, index], crecv.at[j, index], ring.sibling).wait_recv()
    own.wait()
    for copy in sent:
        copy.wait_send()


class Swap:
    def __init__(self, section, dp):
        self.peer = {"section": section, "dp": dp}
        self.stays = section == lax.axis_index("section")

    def greet(self, sem):
        @pl.when(jnp.logical_not(self.stays))
        def _():
            pl.semaphore_signal(sem, inc=1, device_id=self.peer, device_id_type=MESH)

    def start(self, src, dst, sems):
        self.local = pltpu.make_async_copy(src, dst, sems.at[0])
        self.remote = remote(src, dst, sems.at[1], sems.at[2], self.peer)

        @pl.when(self.stays)
        def _():
            self.local.start()

        @pl.when(jnp.logical_not(self.stays))
        def _():
            self.remote.start()

    def wait(self):
        @pl.when(self.stays)
        def _():
            self.local.wait()

        @pl.when(jnp.logical_not(self.stays))
        def _():
            self.remote.wait()


def swap_down(dims, count):
    size = dims[0] * dims[1] * dims[2]
    half, step = size // 2, size // 2 // count
    sec, dp = lax.axis_index("section"), lax.axis_index("dp")
    return Swap(lax.rem(dp, half) // step, dp // half * half + sec * step + lax.rem(dp, step))


def swap_up(dims, count):
    step = dims[0] * dims[1] * dims[2] // count
    sec, dp = lax.axis_index("section"), lax.axis_index("dp")
    return Swap(dp // step, sec * step + lax.rem(dp, step))


def weights_kernel(
    dims, count, a_ref, b_ref, keep_ref, give_ref, out_ref, own_ref, other_ref, hsend, hrecv, asems, bsems, *sems
):
    ring = Ring(dims)
    down, up = swap_down(dims, count), swap_up(dims, count)
    start_barrier(ring.peers, (down, up))
    rows, high = a_ref.shape[0], b_ref.shape[0]
    half = rows // 2
    down.start(a_ref, own_ref.at[pl.ds(rows, rows)], asems)
    up.start(b_ref, own_ref.at[pl.ds(2 * rows, high)], bsems)
    copy = remote(give_ref, other_ref, hsend, hrecv, ring.rows[dims[0] // 2 - 1])
    copy.start()
    copy.wait_recv()
    both = keep_ref[...].astype(F32) + other_ref[...].astype(F32)
    block = jnp.concatenate([both[:half], b_ref[...].astype(F32)[:half]], axis=0)
    own_ref[pl.ds(0, rows)] = block.astype(own_ref.dtype)
    down.wait()
    up.wait()
    spread(ring, own_ref, out_ref, sems)
    copy.wait_send()


def gather_weights(a, b, keep, give, collective_id, dims=DP, count=CALLS):
    rows = 2 * a.shape[0] + b.shape[0]
    dma = pltpu.SemaphoreType.DMA
    vmem = pl.BlockSpec(memory_space=pltpu.VMEM)
    return pl.pallas_call(
        functools.partial(weights_kernel, dims, count),
        out_shape=jax.ShapeDtypeStruct(dims + (rows, a.shape[1]), a.dtype),
        in_specs=[vmem] * 4,
        out_specs=pl.BlockSpec(memory_space=pl.ANY),
        scratch_shapes=[
            pltpu.VMEM((rows, a.shape[1]), a.dtype),
            pltpu.VMEM(give.shape, give.dtype),
            dma,
            dma,
            dma((3,)),
            dma((3,)),
        ]
        + ring_sems(dims),
        compiler_params=pltpu.CompilerParams(collective_id=collective_id, has_side_effects=True),
    )(a, b, keep, give)


def middle_kernel(
    dims,
    secs,
    gram_ref,
    proj_ref,
    gall_ref,
    pall_ref,
    landing,
    total_ref,
    send1,
    recv1,
    send2,
    recv2,
    local_sem,
    across_send,
    across_recv,
    xsend,
    xrecv,
    *sems,
):
    ring = Ring(dims)
    count, width = secs[0] * secs[1], secs[1]
    me = lax.axis_index("section")
    y0, x0 = me // width, lax.rem(me, width)
    peers = [{"section": lax.rem(me + j, count)} for j in range(1, count)]
    across = {"section": (1 - y0) * width + x0}
    beside = [{"section": y0 * width + lax.rem(x0 + j, width)} for j in range(1, width)]
    start_barrier(ring.peers + peers)
    sent = []

    def push(*what):
        copy = remote(*what)
        copy.start()
        sent.append(copy)

    for j in range(1, count):
        push(gram_ref.at[lax.rem(me + j, count)], landing.at[me], send1.at[j], recv1.at[j], peers[j - 1])
    total = gram_ref[me].astype(F32)
    for j in range(1, count):
        source = lax.rem(me + count - j, count)
        block = landing.at[source]
        remote(block, block, send1.at[j], recv1.at[j], peers[j - 1]).wait_recv()
        total = total + landing[source].astype(F32)
    total_ref[me] = total.astype(total_ref.dtype)
    for j in range(1, count):
        push(total_ref.at[me], total_ref.at[me], send2.at[j], recv2.at[j], peers[j - 1])
    own = pltpu.make_async_copy(proj_ref, pall_ref.at[y0, x0], local_sem)
    own.start()
    push(proj_ref, pall_ref.at[y0, x0], across_send, across_recv, across)
    for j in range(1, width):
        push(proj_ref, pall_ref.at[y0, x0], xsend.at[0, j], xrecv.at[0, j], beside[j - 1])
    for j in range(1, count):
        block = total_ref.at[lax.rem(me + count - j, count)]
        remote(block, block, send2.at[j], recv2.at[j], peers[j - 1]).wait_recv()

    def forward():
        block = pall_ref.at[1 - y0, x0]
        remote(block, block, across_send, across_recv, across).wait_recv()
        for j in range(1, width):
            push(block, block, xsend.at[1, j], xrecv.at[1, j], beside[j - 1])

    spread(ring, total_ref, gall_ref, sems, forward)
    for h in range(2):
        for j in range(1, width):
            landed = pall_ref.at[y0 if h == 0 else 1 - y0, lax.rem(x0 + width - j, width)]
            remote(landed, landed, xsend.at[h, j], xrecv.at[h, j], beside[j - 1]).wait_recv()
    own.wait()
    for copy in sent:
        copy.wait_send()


def gather_middle(gram, proj, collective_id, dims=DP, secs=SEC):
    dma = pltpu.SemaphoreType.DMA
    count = secs[0] * secs[1]
    anywhere = pl.BlockSpec(memory_space=pl.ANY)
    return pl.pallas_call(
        functools.partial(middle_kernel, dims, secs),
        out_shape=[
            jax.ShapeDtypeStruct(dims + gram.shape, gram.dtype),
            jax.ShapeDtypeStruct(secs + proj.shape, proj.dtype),
        ],
        in_specs=[pl.BlockSpec(memory_space=pltpu.VMEM), anywhere],
        out_specs=[anywhere, anywhere],
        scratch_shapes=[pltpu.VMEM(gram.shape, gram.dtype)] * 2
        + [dma((count,))] * 4
        + [dma, dma, dma, dma((2, secs[1])), dma((2, secs[1]))]
        + ring_sems(dims),
        compiler_params=pltpu.CompilerParams(collective_id=collective_id, has_side_effects=True),
    )(gram, proj)


def gather_sums(ring, x_ref, from_core, moving, landing, rest, from_row, csend, crecv, zsend, zrecv, ysend, yrecv):
    ys, zs, cs = ring.dims
    y0, z0, c0 = ring.y, ring.z, ring.c
    sent = []
    order = []
    for reach in range(zs // 2, -1, -1):
        for offset in {reach, (zs - reach) % zs}:
            order.append(offset)
    order = sorted(set(order), key=lambda o: -min(o, zs - o))
    for offset in order:
        z = lax.rem(z0 + offset, zs)
        copy = remote(
            x_ref.at[:, z, 1 - c0], from_core.at[offset], csend.at[offset], crecv.at[offset], ring.sibling
        )
        copy.start()
        sent.append(copy)

    def core_sum(offset, j):
        z = lax.rem(z0 + offset, zs)
        return x_ref[j, z, c0].astype(F32) + from_core[offset, j].astype(F32)

    ready = set()

    def need(offset):
        if offset not in ready:
            ready.add(offset)
            block = from_core.at[offset]
            remote(block, block, csend.at[offset], crecv.at[offset], ring.sibling).wait_recv()

    totals = {}
    for k in range(zs // 2 + 1):
        for j in range(ys):
            for side in range(2):
                count = hops(zs, j, ys)[side]
                step = k - (zs // 2 - count)
                if step < 0 or step > count:
                    continue
                reach = count - step
                offset = reach if side == 0 else (zs - reach) % zs
                if step:
                    block = landing.at[side, j, step - 1]
                    remote(
                        block, block, zsend.at[side, j, step - 1], zrecv.at[side, j, step - 1], ring.sides[side]
                    ).wait_recv()
                    got = landing[side, j, step - 1].astype(F32)
                else:
                    got = 0.0
                if reach:
                    need(offset)
                    value = core_sum(offset, j) + got
                    moving[side, j, step] = value.astype(moving.dtype)
                    copy = remote(
                        moving.at[side, j, step],
                        landing.at[side, j, step],
                        zsend.at[side, j, step],
                        zrecv.at[side, j, step],
                        ring.sides[side],
                    )
                    copy.start()
                    sent.append(copy)
                else:
                    if j not in totals:
                        need(0)
                        totals[j] = core_sum(0, j) + got
                    else:
                        rest[j] = (totals[j] + got).astype(rest.dtype)
    for i in range(1, ys):
        row = lax.rem(y0 + i, ys)
        copy = remote(rest.at[row], from_row.at[i], ysend.at[i], yrecv.at[i], ring.rows[i - 1])
        copy.start()
        sent.append(copy)
    own = rest[y0].astype(F32)
    for i in range(1, ys):
        block = from_row.at[i]
        remote(block, block, ysend.at[i], yrecv.at[i], ring.rows[i - 1]).wait_recv()
        own = own + from_row[i].astype(F32)
    return own, sent


def finish_kernel(
    dims,
    count,
    x_ref,
    a_ref,
    gain_ref,
    ga_ref,
    gb_ref,
    gg_ref,
    from_core,
    moving,
    landing,
    rest,
    from_row,
    mine,
    got,
    csend,
    crecv,
    zsend,
    zrecv,
    ysend,
    yrecv,
    asems,
    bsems,
    gsend,
    grecv,
    *sems,
):
    ring = Ring(dims)
    down, up = swap_down(dims, count), swap_up(dims, count)
    me = lax.axis_index("section")
    peers = [{"section": lax.rem(me + j, count)} for j in range(1, count)]
    start_barrier(ring.peers + peers, (down, up))
    own, sent = gather_sums(
        ring, x_ref, from_core, moving, landing, rest, from_row, csend, crecv, zsend, zrecv, ysend, yrecv
    )
    mine[...] = own.astype(mine.dtype)
    rows, rank = a_ref.shape
    high = mine.shape[0] - rows
    low_part, high_part = pl.ds(0, rows), pl.ds(rows, high)
    up.start(mine.at[high_part], got.at[high_part], bsems)
    down.start(mine.at[low_part], got.at[low_part], asems)
    up.wait()

    def gains():
        down.wait()
        w = got[low_part].astype(F32)
        ga_ref[...] = w * gain_ref[...]
        prod = w * a_ref[...].astype(F32)
        if rank > rows:
            prod = jnp.concatenate([prod, jnp.zeros((rank - rows, rank), F32)], axis=0)
        line = lax.dot_general(
            jnp.ones((8, rank), F32), prod, NT, precision=lax.Precision.HIGHEST, preferred_element_type=F32
        )
        gg_ref[me] = line.astype(BF).astype(F32)
        for j in range(1, count):
            copy = remote(gg_ref.at[me], gg_ref.at[me], gsend.at[j], grecv.at[j], peers[j - 1])
            copy.start()
            sent.append(copy)

    spread(ring, got.at[high_part], gb_ref, sems, gains)
    for j in range(1, count):
        block = gg_ref.at[lax.rem(me + count - j, count)]
        remote(block, block, gsend.at[j], grecv.at[j], peers[j - 1]).wait_recv()
    for copy in sent:
        copy.wait_send()


def finish(x, a, gain, collective_id, dims=DP, count=CALLS):
    ys, zs, cs = dims
    block = x.shape[1:]
    high = block[0] - a.shape[0]
    x = x.reshape(dims + block)
    dma = pltpu.SemaphoreType.DMA
    half = zs // 2
    vmem = pl.BlockSpec(memory_space=pltpu.VMEM)
    return pl.pallas_call(
        functools.partial(finish_kernel, dims, count),
        out_shape=[
            jax.ShapeDtypeStruct(a.shape, F32),
            jax.ShapeDtypeStruct(dims + (high, block[1]), BF),
            jax.ShapeDtypeStruct((count, 8, block[1]), F32),
        ],
        in_specs=[vmem] * 3,
        out_specs=[vmem, pl.BlockSpec(memory_space=pl.ANY), vmem],
        scratch_shapes=[
            pltpu.VMEM((zs, ys) + block, x.dtype),
            pltpu.VMEM((2, ys, half) + block, x.dtype),
            pltpu.VMEM((2, ys, half) + block, x.dtype),
            pltpu.VMEM((ys,) + block, x.dtype),
            pltpu.VMEM((ys,) + block, x.dtype),
            pltpu.VMEM(block, x.dtype),
            pltpu.VMEM(block, x.dtype),
            dma((zs,)),
            dma((zs,)),
            dma((2, ys, half)),
            dma((2, ys, half)),
            dma((ys,)),
            dma((ys,)),
            dma((3,)),
            dma((3,)),
            dma((count,)),
            dma((count,)),
        ]
        + ring_sems(dims),
        compiler_params=pltpu.CompilerParams(
            collective_id=collective_id, has_side_effects=True, vmem_limit_bytes=40 * 2**20
        ),
    )(x, a, gain)


def dot(a, b):
    return jnp.dot(a, b, preferred_element_type=F32)


def dot_nt(a, b):
    return lax.dot_general(a, b, NT, preferred_element_type=F32)


def solve_kernel(
    proj_ref,
    e2_ref,
    gram_ref,
    et_ref,
    ct_ref,
    a1_ref,
    a2_ref,
    bt_ref,
    out_ref,
    ge_ref,
    r_ref,
    v_ref,
    w_ref,
    hb_ref,
    h_ref,
    acc_ref,
):
    tokens, rank = r_ref.shape[1:]
    cols = et_ref.shape[0]
    scale = 1.0 / (2 * cols * CALLS)

    def gram(t, pos):
        return gram_ref[14 * t + pos if 2 * t < CALLS else 16 * (CALLS - 1 - t) + pos + 1]

    e2 = e2_ref[:, :1]
    h2 = e2
    invs = []
    for s in range(CALLS):
        pre = proj_ref[s, :, :rank].astype(F32)
        hb = proj_ref[s, :, rank : 2 * rank].astype(F32)
        for t in range(s):
            pre = pre + dot(r_ref[t], gram(t, 2 * s - 1))
            hb = hb + dot(r_ref[t], gram(t, 2 * s))
        inv = lax.rsqrt((e2 + h2) * scale + EPS)
        invs.append(inv)
        r = (pre * inv).astype(BF)
        r_ref[s] = r
        rn = dot(r, gram(s, 2 * s))
        h2 = h2 + jnp.sum(r.astype(F32) * (2.0 * hb + rn), axis=1, keepdims=True)
        hb_ref[s] = hb + rn

    lane = lax.broadcasted_iota(jnp.int32, (tokens, rank), 1)
    kap = jnp.zeros((tokens, 1), F32)
    kmat = jnp.zeros((tokens, rank), F32)
    for s in reversed(range(CALLS)):
        u = proj_ref[s, :, 2 * rank :].astype(F32) - kap * hb_ref[s]
        for t in range(s + 1, CALLS):
            u = u + dot_nt(v_ref[t], gram(s, 2 * t - 1)) + dot_nt(w_ref[t], gram(s, 2 * t))
        u = u.astype(BF).astype(F32)
        r = r_ref[s].astype(F32)
        inv = invs[s]
        q = jnp.sum(u * r, axis=1, keepdims=True) * scale
        k = inv * inv * q
        v_ref[s] = (inv * u).astype(BF)
        w_ref[s] = (-kap * r).astype(BF)
        kmat = jnp.where(lane == s, k, kmat)
        kap = kap + k

    unit = (
        lax.broadcasted_iota(jnp.int32, (CALLS, rank), 0) == lax.broadcasted_iota(jnp.int32, (CALLS, rank), 1)
    ).astype(F32)
    krows = lax.dot_general(unit, kmat, NT, precision=lax.Precision.HIGHEST, preferred_element_type=F32)

    quarter, eighth = cols // 4, cols // 8
    filler = jnp.zeros((out_ref.shape[1] - quarter - eighth, rank), F32)
    h_ref[0] = et_ref[...]
    for t in range(CALLS):
        h = h_ref[t]
        top = dot(h, v_ref[t]).astype(BF)
        low = dot(et_ref[...], v_ref[t]).astype(BF)
        for j in range(4):
            out_ref[t * 4 + j, :quarter] = top[j * quarter : (j + 1) * quarter]
            out_ref[CALLS * 4 + t * 4 + j, :quarter] = low[j * quarter : (j + 1) * quarter]
        if t + 1 < CALLS:
            h_ref[t + 1] = (h.astype(F32) + dot_nt(bt_ref[t], r_ref[t])).astype(BF)
    back = ct_ref[...]
    acc_ref[...] = jnp.zeros(acc_ref.shape, F32)
    for t in reversed(range(CALLS)):
        part = dot(back, r_ref[t])
        for j in range(8):
            piece = jnp.concatenate([part[j * eighth : (j + 1) * eighth], filler], axis=0)
            out_ref[t * 8 + j, quarter:] = piece.astype(BF)
        krow = krows[t : t + 1]
        step = dot_nt(a1_ref[t], v_ref[t]) - krow * h_ref[t].astype(F32)
        back = (back.astype(F32) + step).astype(BF)
        acc_ref[...] += dot_nt(a2_ref[t], v_ref[t]) - krow * et_ref[...].astype(F32)
    ge_ref[...] = (acc_ref[...] + back.astype(F32)).astype(BF)


def solve(proj, e2, gram, et, ct, a1, a2, bt):
    cols, tokens = et.shape
    rank = bt.shape[-1]
    vmem = pl.BlockSpec(memory_space=pltpu.VMEM)
    return pl.pallas_call(
        solve_kernel,
        out_shape=[
            jax.ShapeDtypeStruct((64, cols // 4 + 64, rank), BF),
            jax.ShapeDtypeStruct((cols, tokens), BF),
        ],
        in_specs=[vmem] * 8,
        out_specs=[vmem] * 2,
        scratch_shapes=[
            pltpu.VMEM((CALLS, tokens, rank), BF),
            pltpu.VMEM((CALLS, tokens, rank), BF),
            pltpu.VMEM((CALLS, tokens, rank), BF),
            pltpu.VMEM((CALLS, tokens, rank), F32),
            pltpu.VMEM((CALLS, cols, tokens), BF),
            pltpu.VMEM((cols, tokens), F32),
        ],
        compiler_params=pltpu.CompilerParams(vmem_limit_bytes=48 * 2**20),
    )(proj, e2, gram, et, ct, a1, a2, bt)


def per_device(embeds, cotangent, adapter_a, adapter_b, norm_gains):
    sec = lax.axis_index("section")
    dp = lax.axis_index("dp")
    width = embeds.shape[1]
    cols = width // CALLS
    a_own = adapter_a[0]
    quarter, rank = a_own.shape
    eighth = quarter // 2
    b_pad = jnp.pad(adapter_b[0].T, ((0, 64 - eighth), (0, 0)))
    gain = jnp.where(sec % 2 == 0, norm_gains[0], norm_gains[1])
    gain_rows = lax.dynamic_slice_in_dim(gain, dp * quarter, quarter, 0)
    gain_rows = jnp.broadcast_to(gain_rows[:, None], (quarter, rank))
    a_scaled = (a_own.astype(F32) * gain_rows).astype(BF)
    first, second = (jnp.pad(a_scaled[i : i + eighth], ((0, 64 - eighth), (0, 0))) for i in (0, eighth))
    upper = dp < 32
    sheet = gather_weights(
        a_scaled, b_pad, jnp.where(upper, first, second), jnp.where(upper, second, first), 0
    )
    sheet = sheet.reshape(64, 2 * quarter + 64, rank)
    pmat = sheet[:, :eighth].reshape(2, 32, eighth, rank).transpose(1, 0, 2, 3).reshape(width, rank)
    up = sheet[:, eighth:quarter].reshape(width, rank)
    parts = sheet[:, quarter : 2 * quarter].reshape(2, CALLS, cols, rank)
    bt_cols = sheet[:, 2 * quarter : 2 * quarter + eighth].reshape(CALLS, cols, rank)

    lead, spot = dp // 16, dp % 16
    early = spot < 15 - 2 * lead
    row = jnp.where(early, lead, CALLS - 1 - lead)
    pos = jnp.where(early, 2 * lead + spot, spot - 1)
    col = (pos + 1) // 2
    right = jnp.where(pos % 2 == 0, bt_cols[col], parts[0, col])
    gpart = lax.dot_general(bt_cols[row], right, (((0,), (0,)), ((), ())), preferred_element_type=F32)
    gpart = gpart.astype(BF).reshape(CALLS, 16, rank)
    proj = jnp.concatenate([dot(embeds, jnp.concatenate([pmat, up], axis=1)), dot(cotangent, up)], axis=1)
    gram, proj = gather_middle(gpart, proj.astype(BF), 1)
    gram = gram.reshape(64, rank, rank)
    proj = proj.reshape(CALLS, embeds.shape[0], 3 * rank)

    esq = embeds.astype(F32)
    e2 = jnp.broadcast_to(jnp.sum(esq * esq, axis=1, keepdims=True), (embeds.shape[0], rank))
    et = lax.dynamic_slice_in_dim(embeds, sec * cols, cols, 1).T
    ct = lax.dynamic_slice_in_dim(cotangent, sec * cols, cols, 1).T
    terms, ge = solve(proj, e2, gram, et, ct, parts[0], parts[1], bt_cols)

    grad_a, gb, gains = finish(terms, a_own, gain_rows, 2)
    grad_gain = jnp.sum(gains.reshape(CALLS // 2, 2, 8, rank)[:, :, 0, :quarter], axis=0)
    grad_b = gb.reshape(64, 64, rank)[:, :eighth].reshape(width, rank)
    return (grad_a[None], grad_b.T.astype(F32)[None], grad_gain, ge.T)


def solution(mesh):
    in_specs = (
        P("dp", None),
        P("dp", None),
        P("section", "dp", None),
        P("section", None, "dp"),
        P(),
    )
    out_specs = (
        P("section", "dp", None),
        P("section", None, None),
        P(None, "dp"),
        P("dp", "section"),
    )
    return jax.shard_map(per_device, mesh=mesh, in_specs=in_specs, out_specs=out_specs, check_vma=False)
```

```python
import functools

import jax
import jax.numpy as jnp
from jax import lax
from jax.experimental import pallas as pl
from jax.experimental.pallas import tpu as pltpu
from jax.sharding import PartitionSpec as P

EPS = 1e-05
CALLS = 8
DP = (4, 8, 2)
SEC = (2, 4)
BF = jnp.bfloat16
F32 = jnp.float32
MESH = pl.DeviceIdType.MESH
NT = (((1,), (1,)), ((), ()))


class Entry:
    def __init__(self, peers, swaps=()):
        self.sem = pltpu.get_barrier_semaphore()
        self.count = len(peers)
        for peer in peers:
            pl.semaphore_signal(self.sem, inc=1, device_id=peer, device_id_type=MESH)
        for swap in swaps:
            swap.greet(self.sem)
            self.count = self.count + jnp.where(swap.stays, 0, 1)

    def wait(self):
        pl.semaphore_wait(self.sem, self.count)


def remote(src, dst, send, recv, peer):
    return pltpu.make_async_remote_copy(
        src_ref=src, dst_ref=dst, send_sem=send, recv_sem=recv, device_id=peer, device_id_type=MESH
    )


def hops(zs, stream, ys):
    long_way, short_way = zs // 2, zs - 1 - zs // 2
    return (long_way, short_way) if stream < ys // 2 else (short_way, long_way)


class Ring:
    def __init__(self, dims):
        self.dims = dims
        ys, zs, cs = dims
        me = lax.axis_index("dp")
        self.y, self.z, self.c = me // (zs * cs), lax.rem(me // cs, zs), lax.rem(me, cs)
        self.rows = [self.at(lax.rem(self.y + j, ys), self.z, self.c) for j in range(1, ys)]
        right, left = lax.rem(self.z + 1, zs), lax.rem(self.z + zs - 1, zs)
        self.sides = (self.at(self.y, right, self.c), self.at(self.y, left, self.c))
        self.sibling = self.at(self.y, self.z, 1 - self.c)
        self.peers = self.rows + list(self.sides) + [self.sibling]

    def at(self, y, z, c):
        _, zs, cs = self.dims
        return {"dp": (y * zs + z) * cs + c}


def ring_sems(dims):
    ys, zs, _ = dims
    dma = pltpu.SemaphoreType.DMA
    return [
        dma,
        dma((ys,)),
        dma((ys,)),
        dma((2, ys, zs // 2)),
        dma((2, ys, zs // 2)),
        dma((ys, zs)),
        dma((ys, zs)),
    ]


class Spread:
    def __init__(self, ring, src, out_ref, sems):
        self.ring, self.src, self.out, self.sems = ring, src, out_ref, sems
        self.sent = []
        ys = ring.dims[0]
        self.lines = [lax.rem(ring.y + ys - j, ys) for j in range(ys)]

    def push(self, *what):
        copy = remote(*what)
        copy.start()
        self.sent.append(copy)

    def origin(self, side, k):
        zs = self.ring.dims[1]
        return lax.rem(self.ring.z + (zs - k if side == 0 else k), zs)

    def start(self):
        ring = self.ring
        local_sem, ysend, yrecv = self.sems[:3]
        block = self.out.at[ring.y, ring.z, ring.c]
        self.own = pltpu.make_async_copy(self.src, block, local_sem)
        self.own.start()
        for j in range(1, ring.dims[0]):
            self.push(self.src, block, ysend.at[j], yrecv.at[j], ring.rows[j - 1])

    def relay(self, j, side, k):
        ring = self.ring
        zsend, zrecv = self.sems[3:5]
        block = self.out.at[self.lines[j], self.origin(side, k), ring.c]
        src = block if j or k else self.src
        self.push(src, block, zsend.at[side, j, k], zrecv.at[side, j, k], ring.sides[side])

    def share(self, j, z, index):
        ring = self.ring
        csend, crecv = self.sems[5:7]
        block = self.out.at[self.lines[j], z, ring.c]
        src = block if j or index else self.src
        self.push(src, block, csend.at[j, index], crecv.at[j, index], ring.sibling)

    def first(self):
        ring = self.ring
        ys, zs, _ = ring.dims
        ysend, yrecv = self.sems[1:3]
        for j in range(ys):
            if j:
                block = self.out.at[self.lines[j], ring.z, ring.c]
                remote(block, block, ysend.at[j], yrecv.at[j], ring.rows[j - 1]).wait_recv()
            for side in range(2):
                if hops(zs, j, ys)[side]:
                    self.relay(j, side, 0)
            self.share(j, ring.z, 0)

    def step(self, k):
        ring = self.ring
        ys, zs, _ = ring.dims
        zsend, zrecv = self.sems[3:5]
        for j in range(ys):
            for side in range(2):
                count = hops(zs, j, ys)[side]
                if k <= count:
                    z = self.origin(side, k)
                    block = self.out.at[self.lines[j], z, ring.c]
                    remote(
                        block, block, zsend.at[side, j, k - 1], zrecv.at[side, j, k - 1], ring.sides[side]
                    ).wait_recv()
                    if k < count:
                        self.relay(j, side, k)
                    self.share(j, z, zs - k if side == 0 else k)

    def finish(self):
        ring = self.ring
        ys, zs, _ = ring.dims
        csend, crecv = self.sems[5:7]
        for j in range(ys):
            for index in range(zs):
                block = self.out.at[self.lines[j], lax.rem(ring.z + index, zs), 1 - ring.c]
                remote(block, block, csend.at[j, index], crecv.at[j, index], ring.sibling).wait_recv()
        self.own.wait()
        for copy in self.sent:
            copy.wait_send()

    def run(self, between=None):
        self.start()
        self.first()
        if between is not None:
            between()
        for k in range(1, self.ring.dims[1] // 2 + 1):
            self.step(k)
        self.finish()


class Swap:
    def __init__(self, section, dp):
        self.peer = {"section": section, "dp": dp}
        self.stays = section == lax.axis_index("section")

    def greet(self, sem):
        @pl.when(jnp.logical_not(self.stays))
        def _():
            pl.semaphore_signal(sem, inc=1, device_id=self.peer, device_id_type=MESH)

    def start(self, src, dst, sems):
        self.local = pltpu.make_async_copy(src, dst, sems.at[0])
        self.remote = remote(src, dst, sems.at[1], sems.at[2], self.peer)

        @pl.when(self.stays)
        def _():
            self.local.start()

        @pl.when(jnp.logical_not(self.stays))
        def _():
            self.remote.start()

    def wait(self):
        @pl.when(self.stays)
        def _():
            self.local.wait()

        @pl.when(jnp.logical_not(self.stays))
        def _():
            self.remote.wait()


def swap_down(dims, count):
    size = dims[0] * dims[1] * dims[2]
    half, step = size // 2, size // 2 // count
    sec, dp = lax.axis_index("section"), lax.axis_index("dp")
    return Swap(lax.rem(dp, half) // step, dp // half * half + sec * step + lax.rem(dp, step))


def swap_up(dims, count):
    step = dims[0] * dims[1] * dims[2] // count
    sec, dp = lax.axis_index("section"), lax.axis_index("dp")
    return Swap(dp // step, sec * step + lax.rem(dp, step))


def dot(a, b):
    return jnp.dot(a, b, preferred_element_type=F32)


def dot_nt(a, b):
    return lax.dot_general(a, b, NT, preferred_element_type=F32)


def eye(rows, cols, shift=0, kind=BF):
    row = lax.broadcasted_iota(jnp.int32, (rows, cols), 0)
    col = lax.broadcasted_iota(jnp.int32, (rows, cols), 1)
    return (col == row + shift).astype(F32).astype(kind)


def weights_kernel(
    dims,
    count,
    a_ref,
    b_ref,
    gain_ref,
    sec_ref,
    col_ref,
    scaled,
    b_rows,
    give,
    other,
    own_sec,
    own_col,
    hsend,
    hrecv,
    asems,
    bsems,
    *sems,
):
    ring = Ring(dims)
    down, up = swap_down(dims, count), swap_up(dims, count)
    entry = Entry(ring.peers, (down, up))
    rows, rank = a_ref.shape
    high = b_rows.shape[0]
    half = rows // 2
    value = (a_ref[...].astype(F32) * gain_ref[...]).astype(BF)
    scaled[...] = value
    turned = lax.dot_general(eye(high, half), b_ref[...], NT, preferred_element_type=F32)
    b_rows[...] = turned.astype(BF)
    value = value.astype(F32)
    upper = ring.y < dims[0] // 2
    rest = jnp.where(upper, value[half:], value[:half])
    if high > half:
        rest = jnp.concatenate([rest, jnp.zeros((high - half, rank), F32)], axis=0)
    give[...] = rest.astype(BF)
    entry.wait()
    exchange = remote(give, other, hsend, hrecv, ring.rows[dims[0] // 2 - 1])
    exchange.start()
    down.start(scaled, own_col.at[pl.ds(0, rows)], asems)
    up.start(b_rows, own_col.at[pl.ds(rows, high)], bsems)
    exchange.wait_recv()
    both = jnp.where(upper, value[:half], value[half:]) + other[...].astype(F32)[:half]
    own_sec[...] = jnp.concatenate([both, turned[:half]], axis=0).astype(BF)
    first = Spread(ring, own_sec, sec_ref, sems[: len(sems) // 2])
    second = Spread(ring, own_col, col_ref, sems[len(sems) // 2 :])
    first.start()
    first.first()
    last = dims[1] // 2
    first.step(1)
    down.wait()
    up.wait()
    second.start()
    for k in range(2, last + 1):
        first.step(k)
        if k == 2:
            second.first()
        else:
            second.step(k - 2)
    if last < 2:
        second.first()
    for k in range(max(1, last - 1), last + 1):
        second.step(k)
    first.finish()
    second.finish()
    exchange.wait_send()


def gather_weights(a, b, gain, collective_id, dims=DP, count=CALLS, high=64):
    rows, rank = a.shape
    dma = pltpu.SemaphoreType.DMA
    vmem = pl.BlockSpec(memory_space=pltpu.VMEM)
    anywhere = pl.BlockSpec(memory_space=pl.ANY)
    tall = rows + high
    return pl.pallas_call(
        functools.partial(weights_kernel, dims, count),
        out_shape=[
            jax.ShapeDtypeStruct(dims + (rows, rank), BF),
            jax.ShapeDtypeStruct(dims + (tall, rank), BF),
        ],
        in_specs=[vmem] * 3,
        out_specs=[anywhere] * 2,
        scratch_shapes=[pltpu.VMEM((n, rank), BF) for n in (rows, high, high, high, rows, tall)]
        + [dma, dma, dma((3,)), dma((3,))]
        + ring_sems(dims) * 2,
        compiler_params=pltpu.CompilerParams(
            collective_id=collective_id, has_side_effects=True, vmem_limit_bytes=16 * 2**20
        ),
    )(a, b, gain)


def middle_kernel(
    dims,
    secs,
    gram_ref,
    proj_ref,
    e_ref,
    c_ref,
    gall_ref,
    pall_ref,
    et_ref,
    ct_ref,
    e2_ref,
    landing,
    total_ref,
    send1,
    recv1,
    send2,
    recv2,
    local_sem,
    across_send,
    across_recv,
    xsend,
    xrecv,
    *sems,
):
    ring = Ring(dims)
    count, width = secs[0] * secs[1], secs[1]
    me = lax.axis_index("section")
    y0, x0 = me // width, lax.rem(me, width)
    peers = [{"section": lax.rem(me + j, count)} for j in range(1, count)]
    across = {"section": (1 - y0) * width + x0}
    beside = [{"section": y0 * width + lax.rem(x0 + j, width)} for j in range(1, width)]
    entry = Entry(ring.peers + peers)
    entry.wait()
    sent = []

    def push(*what):
        copy = remote(*what)
        copy.start()
        sent.append(copy)

    for j in range(1, count):
        push(gram_ref.at[lax.rem(me + j, count)], landing.at[me], send1.at[j], recv1.at[j], peers[j - 1])
    cols, tokens = et_ref.shape
    odd = 64 if cols % 128 else 0
    begin = me * cols
    shift = begin - begin // 128 * 128
    window = pl.ds(pl.multiple_of(begin // 128 * 128, 128), cols + odd)
    pick = eye(cols, cols + odd, shift)
    et_ref[...] = dot_nt(pick, e_ref[:, window]).astype(BF)
    ct_ref[...] = dot_nt(pick, c_ref[:, window]).astype(BF)
    square = jnp.zeros((tokens, 128), F32)
    for i in range(e_ref.shape[1] // 128):
        piece = e_ref[:, i * 128 : (i + 1) * 128].astype(F32)
        square = square + piece * piece
    e2_ref[...] = jnp.broadcast_to(jnp.sum(square, axis=1, keepdims=True), (tokens, 128))
    total = gram_ref[me].astype(F32)
    for j in range(1, count):
        source = lax.rem(me + count - j, count)
        block = landing.at[source]
        remote(block, block, send1.at[j], recv1.at[j], peers[j - 1]).wait_recv()
        total = total + landing[source].astype(F32)
    total_ref[me] = total.astype(total_ref.dtype)
    for j in range(1, count):
        push(total_ref.at[me], total_ref.at[me], send2.at[j], recv2.at[j], peers[j - 1])
    own = pltpu.make_async_copy(proj_ref, pall_ref.at[y0, x0], local_sem)
    own.start()
    push(proj_ref, pall_ref.at[y0, x0], across_send, across_recv, across)
    for j in range(1, width):
        push(proj_ref, pall_ref.at[y0, x0], xsend.at[0, j], xrecv.at[0, j], beside[j - 1])
    for j in range(1, count):
        block = total_ref.at[lax.rem(me + count - j, count)]
        remote(block, block, send2.at[j], recv2.at[j], peers[j - 1]).wait_recv()

    def forward():
        block = pall_ref.at[1 - y0, x0]
        remote(block, block, across_send, across_recv, across).wait_recv()
        for j in range(1, width):
            push(block, block, xsend.at[1, j], xrecv.at[1, j], beside[j - 1])

    Spread(ring, total_ref, gall_ref, sems).run(forward)
    for h in range(2):
        for j in range(1, width):
            landed = pall_ref.at[y0 if h == 0 else 1 - y0, lax.rem(x0 + width - j, width)]
            remote(landed, landed, xsend.at[h, j], xrecv.at[h, j], beside[j - 1]).wait_recv()
    own.wait()
    for copy in sent:
        copy.wait_send()


def gather_middle(gram, proj, embeds, cotangent, collective_id, dims=DP, secs=SEC):
    dma = pltpu.SemaphoreType.DMA
    count = secs[0] * secs[1]
    tokens, width = embeds.shape
    vmem = pl.BlockSpec(memory_space=pltpu.VMEM)
    anywhere = pl.BlockSpec(memory_space=pl.ANY)
    return pl.pallas_call(
        functools.partial(middle_kernel, dims, secs),
        out_shape=[
            jax.ShapeDtypeStruct(dims + gram.shape, gram.dtype),
            jax.ShapeDtypeStruct(secs + proj.shape, proj.dtype),
            jax.ShapeDtypeStruct((width // count, tokens), BF),
            jax.ShapeDtypeStruct((width // count, tokens), BF),
            jax.ShapeDtypeStruct((tokens, 128), F32),
        ],
        in_specs=[vmem, anywhere, vmem, vmem],
        out_specs=[anywhere, anywhere, vmem, vmem, vmem],
        scratch_shapes=[pltpu.VMEM(gram.shape, gram.dtype)] * 2
        + [dma((count,))] * 4
        + [dma, dma, dma, dma((2, secs[1])), dma((2, secs[1]))]
        + ring_sems(dims),
        compiler_params=pltpu.CompilerParams(
            collective_id=collective_id, has_side_effects=True, vmem_limit_bytes=32 * 2**20
        ),
    )(gram, proj, embeds, cotangent)


class Scatter:
    def __init__(self, ring, x_ref, rows, buffers, sems):
        self.ring, self.x, self.rows = ring, x_ref, rows
        self.from_core, self.moving, self.landing, self.rest, self.from_row = buffers
        self.sems = sems
        self.sent = []
        self.ready = set()
        self.totals = {}

    def push(self, *what):
        copy = remote(*what)
        copy.start()
        self.sent.append(copy)

    def start(self):
        ring = self.ring
        zs = ring.dims[1]
        csend, crecv = self.sems[:2]
        for offset in sorted(range(zs), key=lambda o: -min(o, zs - o)):
            z = lax.rem(ring.z + offset, zs)
            self.push(
                self.x.at[:, z, 1 - ring.c, self.rows],
                self.from_core.at[offset],
                csend.at[offset],
                crecv.at[offset],
                ring.sibling,
            )

    def need(self, offset):
        csend, crecv = self.sems[:2]
        if offset not in self.ready:
            self.ready.add(offset)
            block = self.from_core.at[offset]
            remote(block, block, csend.at[offset], crecv.at[offset], self.ring.sibling).wait_recv()

    def local_sum(self, offset, j):
        self.need(offset)
        ring = self.ring
        z = lax.rem(ring.z + offset, ring.dims[1])
        return self.x[j, z, ring.c, self.rows].astype(F32) + self.from_core[offset, j].astype(F32)

    def step(self, k):
        ring = self.ring
        ys, zs, _ = ring.dims
        zsend, zrecv = self.sems[2:4]
        for j in range(ys):
            for side in range(2):
                count = hops(zs, j, ys)[side]
                step = k - (zs // 2 - count)
                if step < 0:
                    continue
                reach = count - step
                offset = reach if side == 0 else (zs - reach) % zs
                got = 0.0
                if step:
                    spot = (side, j, step - 1)
                    block = self.landing.at[spot]
                    remote(block, block, zsend.at[spot], zrecv.at[spot], ring.sides[side]).wait_recv()
                    got = self.landing[spot].astype(F32)
                if reach:
                    spot = (side, j, step)
                    self.moving[spot] = (self.local_sum(offset, j) + got).astype(BF)
                    self.push(
                        self.moving.at[spot], self.landing.at[spot], zsend.at[spot], zrecv.at[spot], ring.sides[side]
                    )
                elif j not in self.totals:
                    self.totals[j] = self.local_sum(0, j) + got
                else:
                    self.rest[j] = (self.totals[j] + got).astype(BF)

    def rows_start(self):
        ring = self.ring
        ys = ring.dims[0]
        ysend, yrecv = self.sems[4:6]
        for i in range(1, ys):
            row = lax.rem(ring.y + i, ys)
            self.push(self.rest.at[row], self.from_row.at[i], ysend.at[i], yrecv.at[i], ring.rows[i - 1])

    def rows_finish(self):
        ring = self.ring
        ysend, yrecv = self.sems[4:6]
        own = self.rest[ring.y].astype(F32)
        for i in range(1, ring.dims[0]):
            block = self.from_row.at[i]
            remote(block, block, ysend.at[i], yrecv.at[i], ring.rows[i - 1]).wait_recv()
            own = own + self.from_row[i].astype(F32)
        return own

    def finish(self):
        for copy in self.sent:
            copy.wait_send()


def scatter_buffers(dims, rows, rank):
    ys, zs, _ = dims
    block = (rows, rank)
    shapes = [(zs, ys), (2, ys, zs // 2), (2, ys, zs // 2), (ys,), (ys,)]
    return [pltpu.VMEM(shape + block, BF) for shape in shapes]


def scatter_sems(dims):
    ys, zs, _ = dims
    dma = pltpu.SemaphoreType.DMA
    return [dma((zs,)), dma((zs,)), dma((2, ys, zs // 2)), dma((2, ys, zs // 2)), dma((ys,)), dma((ys,))]


def finish_kernel(dims, count, compute, inputs, *refs):
    given, refs = refs[:inputs], refs[inputs:]
    a_ref, gain_ref, ga_ref, gb_ref, gg_ref, ge_ref, x_ref, mine_low, got_low, mine_high, got_high = refs[:11]
    low_buffers, high_buffers = refs[11:16], refs[16:21]
    low_sems, high_sems = refs[21:27], refs[27:33]
    asems, bsems, gsend, grecv = refs[33:37]
    ring_part = refs[37:44]
    scratch = refs[44:]
    ring = Ring(dims)
    down, up = swap_down(dims, count), swap_up(dims, count)
    me = lax.axis_index("section")
    peers = [{"section": lax.rem(me + j, count)} for j in range(1, count)]
    entry = Entry(ring.peers + peers, (down, up))
    rows, rank = a_ref.shape
    high = got_high.shape[0]
    upper = Scatter(ring, x_ref, pl.ds(rows, high), high_buffers, high_sems)
    lower = Scatter(ring, x_ref, pl.ds(0, rows), low_buffers, low_sems)
    work = compute(given, x_ref, ge_ref, scratch)
    work.ups()
    entry.wait()
    upper.start()
    upper.step(0)
    work.downs()
    lower.start()
    last = dims[1] // 2
    for k in range(1, last + 1):
        upper.step(k)
        if k > 1 or last == 1:
            lower.step(max(k - 2, 0))
    upper.rows_start()
    if last > 1:
        lower.step(last - 1)
    mine_high[...] = upper.rows_finish().astype(BF)
    up.start(mine_high, got_high, bsems)
    lower.step(last)
    lower.rows_start()
    work.rest()
    mine_low[...] = lower.rows_finish().astype(BF)
    down.start(mine_low, got_low, asems)
    up.wait()
    gather = Spread(ring, got_high, gb_ref, ring_part)
    gather.start()
    gather.first()
    down.wait()
    w = got_low[...].astype(F32)
    ga_ref[...] = w * gain_ref[...]
    prod = w * a_ref[...].astype(F32)
    if rank > rows:
        prod = jnp.concatenate([prod, jnp.zeros((rank - rows, rank), F32)], axis=0)
    line = lax.dot_general(
        jnp.ones((8, rank), F32), prod, NT, precision=lax.Precision.HIGHEST, preferred_element_type=F32
    )
    gg_ref[me] = line.astype(BF).astype(F32)
    sent = []
    for j in range(1, count):
        copy = remote(gg_ref.at[me], gg_ref.at[me], gsend.at[j], grecv.at[j], peers[j - 1])
        copy.start()
        sent.append(copy)
    for k in range(1, last + 1):
        gather.step(k)
    gather.finish()
    for j in range(1, count):
        block = gg_ref.at[lax.rem(me + count - j, count)]
        remote(block, block, gsend.at[j], grecv.at[j], peers[j - 1]).wait_recv()
    for copy in sent:
        copy.wait_send()
    upper.finish()
    lower.finish()


def finish(given, a, gain, ge_shape, compute, scratch, collective_id, dims=DP, count=CALLS, high=64):
    rows, rank = a.shape
    dma = pltpu.SemaphoreType.DMA
    vmem = pl.BlockSpec(memory_space=pltpu.VMEM)
    return pl.pallas_call(
        functools.partial(finish_kernel, dims, count, compute, len(given)),
        out_shape=[
            jax.ShapeDtypeStruct(a.shape, F32),
            jax.ShapeDtypeStruct(dims + (high, rank), BF),
            jax.ShapeDtypeStruct((count, 8, rank), F32),
            jax.ShapeDtypeStruct(ge_shape, BF),
        ],
        in_specs=[vmem] * (len(given) + 2),
        out_specs=[vmem, pl.BlockSpec(memory_space=pl.ANY), vmem, vmem],
        scratch_shapes=[pltpu.VMEM(dims + (rows + high, rank), BF)]
        + [pltpu.VMEM((n, rank), BF) for n in (rows, rows, high, high)]
        + scatter_buffers(dims, rows, rank)
        + scatter_buffers(dims, high, rank)
        + scatter_sems(dims) * 2
        + [dma((3,)), dma((3,)), dma((count,)), dma((count,))]
        + ring_sems(dims)
        + scratch,
        compiler_params=pltpu.CompilerParams(
            collective_id=collective_id, has_side_effects=True, vmem_limit_bytes=48 * 2**20
        ),
    )(*given, a, gain)


class Solver:
    def __init__(self, given, x_ref, ge_ref, scratch):
        self.given, self.x, self.ge = given, x_ref, ge_ref
        self.r, self.v, self.w, self.hb, self.h, self.acc = scratch
        self.col = given[5]

    def down_rows(self, half, t):
        quarter = self.h.shape[1] // 4
        first = half * 4 * CALLS + t * 4
        return jnp.concatenate([self.col[first + j, :quarter] for j in range(4)], axis=0)

    def up_rows(self, t):
        quarter = self.h.shape[1] // 4
        eighth = quarter // 2
        pieces = [self.col[t * 8 + j, quarter:].astype(F32)[:eighth] for j in range(8)]
        return jnp.concatenate(pieces, axis=0).astype(BF)

    def put(self, index, rows, value):
        self.x[index // 16, index // 2 % 8, index % 2, rows] = value

    def ups(self):
        proj_ref, e2_ref, gram_ref, et_ref, ct_ref, _ = self.given
        r_ref, v_ref, w_ref, hb_ref, h_ref, acc_ref = self.r, self.v, self.w, self.hb, self.h, self.acc
        tokens, rank = r_ref.shape[1:]
        cols = et_ref.shape[0]
        scale = 1.0 / (2 * cols * CALLS)

        def gram(t, pos):
            return gram_ref[14 * t + pos if 2 * t < CALLS else 16 * (CALLS - 1 - t) + pos + 1]

        e2 = e2_ref[:, :1]
        h2 = e2
        invs = []
        for s in range(CALLS):
            pre = proj_ref[s, :, :rank].astype(F32)
            hb = proj_ref[s, :, rank : 2 * rank].astype(F32)
            for t in range(s):
                pre = pre + dot(r_ref[t], gram(t, 2 * s - 1))
                hb = hb + dot(r_ref[t], gram(t, 2 * s))
            inv = lax.rsqrt((e2 + h2) * scale + EPS)
            invs.append(inv)
            r = (pre * inv).astype(BF)
            r_ref[s] = r
            rn = dot(r, gram(s, 2 * s))
            h2 = h2 + jnp.sum(r.astype(F32) * (2.0 * hb + rn), axis=1, keepdims=True)
            hb_ref[s] = hb + rn

        lane = lax.broadcasted_iota(jnp.int32, (tokens, rank), 1)
        kap = jnp.zeros((tokens, 1), F32)
        kmat = jnp.zeros((tokens, rank), F32)
        for s in reversed(range(CALLS)):
            u = proj_ref[s, :, 2 * rank :].astype(F32) - kap * hb_ref[s]
            for t in range(s + 1, CALLS):
                u = u + dot_nt(v_ref[t], gram(s, 2 * t - 1)) + dot_nt(w_ref[t], gram(s, 2 * t))
            u = u.astype(BF).astype(F32)
            r = r_ref[s].astype(F32)
            inv = invs[s]
            q = jnp.sum(u * r, axis=1, keepdims=True) * scale
            k = inv * inv * q
            v_ref[s] = (inv * u).astype(BF)
            w_ref[s] = (-kap * r).astype(BF)
            kmat = jnp.where(lane == s, k, kmat)
            kap = kap + k

        unit = (
            lax.broadcasted_iota(jnp.int32, (CALLS, rank), 0) == lax.broadcasted_iota(jnp.int32, (CALLS, rank), 1)
        ).astype(F32)
        krows = lax.dot_general(unit, kmat, NT, precision=lax.Precision.HIGHEST, preferred_element_type=F32)

        quarter, eighth = cols // 4, cols // 8
        filler = jnp.zeros((64 - eighth, rank), F32)
        h_ref[0] = et_ref[...]
        for t in range(CALLS - 1):
            h_ref[t + 1] = (h_ref[t].astype(F32) + dot_nt(self.up_rows(t), r_ref[t])).astype(BF)
        back = ct_ref[...]
        for t in reversed(range(CALLS)):
            part = dot(back, r_ref[t])
            for j in range(8):
                piece = jnp.concatenate([part[j * eighth : (j + 1) * eighth], filler], axis=0)
                self.put(t * 8 + j, pl.ds(quarter, 64), piece.astype(BF))
            step = dot_nt(self.down_rows(0, t), v_ref[t]) - krows[t : t + 1] * h_ref[t].astype(F32)
            back = (back.astype(F32) + step).astype(BF)
        total = back.astype(F32) - jnp.sum(krows, axis=0, keepdims=True) * et_ref[...].astype(F32)
        acc_ref[...] = total

    def downs(self):
        et_ref = self.given[3]
        quarter = self.h.shape[1] // 4
        for t in range(CALLS):
            for half, source in ((0, self.h[t]), (1, et_ref[...])):
                value = dot(source, self.v[t]).astype(BF)
                for j in range(4):
                    index = half * 4 * CALLS + t * 4 + j
                    self.put(index, pl.ds(0, quarter), value[j * quarter : (j + 1) * quarter])

    def rest(self):
        for t in range(CALLS):
            self.acc[...] += dot_nt(self.down_rows(1, t), self.v[t])
        self.ge[...] = self.acc[...].astype(BF)


def per_device(embeds, cotangent, adapter_a, adapter_b, norm_gains):
    sec = lax.axis_index("section")
    dp = lax.axis_index("dp")
    tokens, width = embeds.shape
    cols = width // CALLS
    a_own = adapter_a[0]
    quarter, rank = a_own.shape
    eighth = quarter // 2
    gain = jnp.where(sec % 2 == 0, norm_gains[0], norm_gains[1])
    gain_rows = lax.dynamic_slice_in_dim(gain, dp * quarter, quarter, 0)
    gain_rows = jnp.broadcast_to(gain_rows[:, None], (quarter, rank))
    own, col = gather_weights(a_own, adapter_b[0], gain_rows, 0)
    own = own.reshape(64, quarter, rank)
    col = col.reshape(64, quarter + 64, rank)
    pmat = own[:, :eighth].reshape(2, 32, eighth, rank).transpose(1, 0, 2, 3).reshape(width, rank)
    up = own[:, eighth:].reshape(width, rank)
    proj = jnp.concatenate([dot(embeds, jnp.concatenate([pmat, up], axis=1)), dot(cotangent, up)], axis=1)

    lead, spot = dp // 16, dp % 16
    early = spot < 15 - 2 * lead
    row = jnp.where(early, lead, CALLS - 1 - lead)
    pos = jnp.where(early, 2 * lead + spot, spot - 1)
    other = (pos + 1) // 2
    bt_of = lambda t: lax.dynamic_slice_in_dim(col, t * 8, 8, 0)[:, quarter : quarter + eighth].reshape(cols, rank)
    a1 = lax.dynamic_slice_in_dim(col, other * 4, 4, 0)[:, :quarter].reshape(cols, rank)
    right = jnp.where(pos % 2 == 0, bt_of(other), a1)
    gpart = lax.dot_general(bt_of(row), right, (((0,), (0,)), ((), ())), preferred_element_type=F32)
    gpart = gpart.astype(BF).reshape(CALLS, 16, rank)
    gram, proj, et, ct, e2 = gather_middle(gpart, proj.astype(BF), embeds, cotangent, 1)
    gram = gram.reshape(64, rank, rank)
    proj = proj.reshape(CALLS, tokens, 3 * rank)

    scratch = [
        pltpu.VMEM((CALLS, tokens, rank), BF),
        pltpu.VMEM((CALLS, tokens, rank), BF),
        pltpu.VMEM((CALLS, tokens, rank), BF),
        pltpu.VMEM((CALLS, tokens, rank), F32),
        pltpu.VMEM((CALLS, cols, tokens), BF),
        pltpu.VMEM((cols, tokens), F32),
    ]
    grad_a, gb, gains, ge = finish(
        (proj, e2, gram, et, ct, col), a_own, gain_rows, (cols, tokens), Solver, scratch, 2
    )
    grad_gain = jnp.sum(gains.reshape(CALLS // 2, 2, 8, rank)[:, :, 0, :quarter], axis=0)
    grad_b = gb.reshape(64, 64, rank)[:, :eighth].reshape(width, rank)
    return (grad_a[None], grad_b.T.astype(F32)[None], grad_gain, ge.T)


def solution(mesh):
    in_specs = (
        P("dp", None),
        P("dp", None),
        P("section", "dp", None),
        P("section", None, "dp"),
        P(),
    )
    out_specs = (
        P("section", "dp", None),
        P("section", None, None),
        P(None, "dp"),
        P("dp", "section"),
    )
    return jax.shard_map(per_device, mesh=mesh, in_specs=in_specs, out_specs=out_specs, check_vma=False)
```

```python
import functools

import jax
import jax.numpy as jnp
from jax import lax
from jax.experimental import pallas as pl
from jax.experimental.pallas import tpu as pltpu
from jax.sharding import PartitionSpec as P

EPS = 1e-05
CALLS = 8
DP = (4, 8, 2)
SEC = (2, 4)
BF = jnp.bfloat16
F32 = jnp.float32
MESH = pl.DeviceIdType.MESH
NT = (((1,), (1,)), ((), ()))


class Entry:
    def __init__(self, peers, swaps=()):
        self.sem = pltpu.get_barrier_semaphore()
        self.count = len(peers)
        for peer in peers:
            pl.semaphore_signal(self.sem, inc=1, device_id=peer, device_id_type=MESH)
        for swap in swaps:
            swap.greet(self.sem)
            self.count = self.count + jnp.where(swap.stays, 0, 1)

    def wait(self):
        pl.semaphore_wait(self.sem, self.count)


def remote(src, dst, send, recv, peer):
    return pltpu.make_async_remote_copy(
        src_ref=src, dst_ref=dst, send_sem=send, recv_sem=recv, device_id=peer, device_id_type=MESH
    )


def hops(zs, stream, ys):
    long_way, short_way = zs // 2, zs - 1 - zs // 2
    return (long_way, short_way) if stream < ys // 2 else (short_way, long_way)


class Ring:
    def __init__(self, dims):
        self.dims = dims
        ys, zs, cs = dims
        me = lax.axis_index("dp")
        self.y, self.z, self.c = me // (zs * cs), lax.rem(me // cs, zs), lax.rem(me, cs)
        self.rows = [self.at(lax.rem(self.y + j, ys), self.z, self.c) for j in range(1, ys)]
        right, left = lax.rem(self.z + 1, zs), lax.rem(self.z + zs - 1, zs)
        self.sides = (self.at(self.y, right, self.c), self.at(self.y, left, self.c))
        self.sibling = self.at(self.y, self.z, 1 - self.c)
        self.peers = self.rows + list(self.sides) + [self.sibling]

    def at(self, y, z, c):
        _, zs, cs = self.dims
        return {"dp": (y * zs + z) * cs + c}


def ring_sems(dims):
    ys, zs, _ = dims
    dma = pltpu.SemaphoreType.DMA
    return [
        dma,
        dma((ys,)),
        dma((ys,)),
        dma((2, ys, zs // 2)),
        dma((2, ys, zs // 2)),
        dma((ys, zs)),
        dma((ys, zs)),
    ]


class Spread:
    def __init__(self, ring, src, out_ref, sems):
        self.ring, self.src, self.out, self.sems = ring, src, out_ref, sems
        self.sent = []
        self.own = None
        ys = ring.dims[0]
        self.lines = [lax.rem(ring.y + ys - j, ys) for j in range(ys)]

    def push(self, *what):
        copy = remote(*what)
        copy.start()
        self.sent.append(copy)

    def origin(self, side, k):
        zs = self.ring.dims[1]
        return lax.rem(self.ring.z + (zs - k if side == 0 else k), zs)

    def start(self):
        ring = self.ring
        local_sem, ysend, yrecv = self.sems[:3]
        block = self.out.at[ring.y, ring.z, ring.c]
        self.own = pltpu.make_async_copy(self.src, block, local_sem)
        self.own.start()
        for j in range(1, ring.dims[0]):
            self.push(self.src, block, ysend.at[j], yrecv.at[j], ring.rows[j - 1])

    def await_own(self):
        pass

    def relay(self, j, side, k):
        ring = self.ring
        zsend, zrecv = self.sems[3:5]
        block = self.out.at[self.lines[j], self.origin(side, k), ring.c]
        src = block if j or k or self.src is None else self.src
        self.push(src, block, zsend.at[side, j, k], zrecv.at[side, j, k], ring.sides[side])

    def share(self, j, z, index):
        ring = self.ring
        csend, crecv = self.sems[5:7]
        block = self.out.at[self.lines[j], z, ring.c]
        src = block if j or index or self.src is None else self.src
        self.push(src, block, csend.at[j, index], crecv.at[j, index], ring.sibling)

    def first(self):
        ring = self.ring
        ys, zs, _ = ring.dims
        ysend, yrecv = self.sems[1:3]
        for j in range(ys):
            if j:
                block = self.out.at[self.lines[j], ring.z, ring.c]
                remote(block, block, ysend.at[j], yrecv.at[j], ring.rows[j - 1]).wait_recv()
            else:
                self.await_own()
            for side in range(2):
                if hops(zs, j, ys)[side]:
                    self.relay(j, side, 0)
            self.share(j, ring.z, 0)

    def step(self, k):
        ring = self.ring
        ys, zs, _ = ring.dims
        zsend, zrecv = self.sems[3:5]
        for j in range(ys):
            for side in range(2):
                count = hops(zs, j, ys)[side]
                if k <= count:
                    z = self.origin(side, k)
                    block = self.out.at[self.lines[j], z, ring.c]
                    remote(
                        block, block, zsend.at[side, j, k - 1], zrecv.at[side, j, k - 1], ring.sides[side]
                    ).wait_recv()
                    if k < count:
                        self.relay(j, side, k)
                    self.share(j, z, zs - k if side == 0 else k)

    def landed(self):
        ring = self.ring
        ys, zs, _ = ring.dims
        csend, crecv = self.sems[5:7]
        for j in range(ys):
            for index in range(zs):
                block = self.out.at[self.lines[j], lax.rem(ring.z + index, zs), 1 - ring.c]
                remote(block, block, csend.at[j, index], crecv.at[j, index], ring.sibling).wait_recv()
        if self.own is not None:
            self.own.wait()

    def drain(self):
        for copy in self.sent:
            copy.wait_send()

    def finish(self):
        self.landed()
        self.drain()


class Fan(Spread):
    def __init__(self, ring, count, out_ref, sems):
        super().__init__(ring, None, out_ref, sems)
        ys, zs, cs = ring.dims
        step = ys * zs * cs // count
        sec, dp = lax.axis_index("section"), lax.axis_index("dp")
        self.call, slot = dp // step, sec * step + lax.rem(dp, step)
        self.stays = self.call == sec
        self.slot = (slot // (zs * cs), lax.rem(slot // cs, zs), lax.rem(slot, cs))
        self.targets, self.sources = [], []
        for i in range(ys):
            y = lax.rem(self.slot[0] + i, ys)
            self.targets.append({"section": self.call, **ring.at(y, *self.slot[1:])})
            place = (self.lines[i] * zs + ring.z) * cs + ring.c
            self.sources.append({"section": place // step, "dp": sec * step + lax.rem(place, step)})

    def greet(self, sem):
        for peer in self.sources[1:]:
            pl.semaphore_signal(sem, inc=1, device_id=peer, device_id_type=MESH)

        @pl.when(jnp.logical_not(self.stays))
        def _():
            pl.semaphore_signal(sem, inc=1, device_id=self.sources[0], device_id_type=MESH)

    def start_from(self, src):
        local_sem, ysend, yrecv = self.sems[:3]
        spot = self.out.at[self.slot]
        self.local = pltpu.make_async_copy(src, spot, local_sem)
        self.cross = remote(src, spot, ysend.at[0], yrecv.at[0], self.targets[0])

        @pl.when(self.stays)
        def _():
            self.local.start()

        @pl.when(jnp.logical_not(self.stays))
        def _():
            self.cross.start()

        for i in range(1, self.ring.dims[0]):
            self.push(src, spot, ysend.at[i], yrecv.at[i], self.targets[i])

    def await_own(self):
        ring = self.ring
        block = self.out.at[ring.y, ring.z, ring.c]
        ysend, yrecv = self.sems[1:3]

        @pl.when(self.stays)
        def _():
            self.local.wait()

        @pl.when(jnp.logical_not(self.stays))
        def _():
            remote(block, block, ysend.at[0], yrecv.at[0], self.targets[0]).wait_recv()

    def drain(self):
        super().drain()

        @pl.when(jnp.logical_not(self.stays))
        def _():
            self.cross.wait_send()


class Swap:
    def __init__(self, section, dp):
        self.peer = {"section": section, "dp": dp}
        self.stays = section == lax.axis_index("section")

    def greet(self, sem):
        @pl.when(jnp.logical_not(self.stays))
        def _():
            pl.semaphore_signal(sem, inc=1, device_id=self.peer, device_id_type=MESH)

    def start(self, src, dst, sems):
        self.local = pltpu.make_async_copy(src, dst, sems.at[0])
        self.remote = remote(src, dst, sems.at[1], sems.at[2], self.peer)

        @pl.when(self.stays)
        def _():
            self.local.start()

        @pl.when(jnp.logical_not(self.stays))
        def _():
            self.remote.start()

    def wait(self):
        @pl.when(self.stays)
        def _():
            self.local.wait()

        @pl.when(jnp.logical_not(self.stays))
        def _():
            self.remote.wait()


def swap_down(dims, count):
    size = dims[0] * dims[1] * dims[2]
    half, step = size // 2, size // 2 // count
    sec, dp = lax.axis_index("section"), lax.axis_index("dp")
    return Swap(lax.rem(dp, half) // step, dp // half * half + sec * step + lax.rem(dp, step))


def swap_up(dims, count):
    step = dims[0] * dims[1] * dims[2] // count
    sec, dp = lax.axis_index("section"), lax.axis_index("dp")
    return Swap(dp // step, sec * step + lax.rem(dp, step))


def dot(a, b):
    return jnp.dot(a, b, preferred_element_type=F32)


def dot_nt(a, b):
    return lax.dot_general(a, b, NT, preferred_element_type=F32)


def eye(rows, cols, shift=0, kind=BF):
    row = lax.broadcasted_iota(jnp.int32, (rows, cols), 0)
    col = lax.broadcasted_iota(jnp.int32, (rows, cols), 1)
    return (col == row + shift).astype(F32).astype(kind)


class Front:
    def __init__(self, sec_ref, col_ref, e_ref, c_ref, wide_ref, et_ref, ct_ref, e2_ref):
        self.sec, self.col, self.e, self.c, self.wide = sec_ref, col_ref, e_ref, c_ref, wide_ref
        self.et, self.ct, self.e2 = et_ref, ct_ref, e2_ref

    def tokens(self):
        cols, tokens = self.et.shape
        odd = 64 if cols % 128 else 0
        begin = lax.axis_index("section") * cols
        start = begin // 128 * 128
        window = pl.ds(pl.multiple_of(start, 128), cols + odd)
        pick = eye(cols, cols + odd, begin - start)
        self.et[...] = dot_nt(pick, self.e[:, window]).astype(BF)
        self.ct[...] = dot_nt(pick, self.c[:, window]).astype(BF)
        square = jnp.zeros((tokens, 128), F32)
        for i in range(self.e.shape[1] // 128):
            piece = self.e[:, i * 128 : (i + 1) * 128].astype(F32)
            square = square + piece * piece
        self.e2[...] = jnp.broadcast_to(jnp.sum(square, axis=1, keepdims=True), (tokens, 128))

    def project(self, out_ref):
        rows, rank = self.sec.shape[3:]
        half = rows // 2
        for i in range(32):
            y, z, c = i // 16, i // 2 % 8, i % 2
            low, high = self.sec[y, z, c].astype(F32), self.sec[y + 2, z, c].astype(F32)
            both = jnp.concatenate([low[:half], high[:half]], axis=0)
            self.wide[i * rows : (i + 1) * rows, :rank] = both.astype(BF)
            low, high = self.sec[i // 8, i % 8, 0].astype(F32), self.sec[i // 8, i % 8, 1].astype(F32)
            both = jnp.concatenate([low[half:], high[half:]], axis=0)
            self.wide[i * rows : (i + 1) * rows, rank:] = both.astype(BF)
        out_ref[:, : 2 * rank] = dot(self.e[...], self.wide[...]).astype(BF)
        out_ref[:, 2 * rank :] = dot(self.c[...], self.wide[:, rank:]).astype(BF)

    def block(self, index):
        return self.col[index // 16, lax.rem(index // 2, 8), lax.rem(index, 2)].astype(F32)

    def gram(self, out_ref):
        quarter = self.et.shape[0] // 4
        eighth = quarter // 2
        dp = lax.axis_index("dp")
        lead, spot = dp // 16, lax.rem(dp, 16)
        early = spot < 15 - 2 * lead
        row = jnp.where(early, lead, CALLS - 1 - lead)
        pos = jnp.where(early, 2 * lead + spot, spot - 1)
        other = (pos + 1) // 2
        even = lax.rem(pos, 2) == 0
        left = jnp.concatenate([self.block(row * 8 + j)[quarter:][:eighth] for j in range(8)], axis=0)
        ups = jnp.concatenate([self.block(other * 8 + j)[quarter:][:eighth] for j in range(8)], axis=0)
        downs = jnp.concatenate([self.block(other * 4 + j)[:quarter] for j in range(4)], axis=0)
        right = jnp.where(even, ups, downs)
        value = lax.dot_general(
            left.astype(BF), right.astype(BF), (((0,), (0,)), ((), ())), preferred_element_type=F32
        )
        out_ref[...] = value.astype(BF)


def front_kernel(dims, secs, make, *refs):
    a_ref, b_ref, gain_ref, e_hbm, c_hbm = refs[:5]
    col_out, gall_ref, pall_ref, et_ref, ct_ref, e2_ref = refs[5:11]
    scaled, b_rows, give, other, own_sec, own_col = refs[11:17]
    sec_ref, col_ref, e_ref, c_ref, wide_ref, proj_ref, gram_ref, landing, total_ref = refs[17:26]
    load_e, load_c, save_col, hsend, hrecv, asems, bsems = refs[26:33]
    gsend, grecv, local_sem, across_send, across_recv, xsend, xrecv = refs[33:40]
    first_sems, second_sems, third_sems = refs[40:47], refs[47:54], refs[54:61]
    ring = Ring(dims)
    count, width = secs[0] * secs[1], secs[1]
    me = lax.axis_index("section")
    y0, x0 = me // width, lax.rem(me, width)
    peers = [{"section": lax.rem(me + j, count)} for j in range(1, count)]
    across = {"section": (1 - y0) * width + x0}
    beside = [{"section": y0 * width + lax.rem(x0 + j, width)} for j in range(1, width)]
    down, up = swap_down(dims, count), swap_up(dims, count)
    entry = Entry(ring.peers + peers, (down, up))
    loads = [pltpu.make_async_copy(e_hbm, e_ref, load_e), pltpu.make_async_copy(c_hbm, c_ref, load_c)]
    for load in loads:
        load.start()
    work = make(sec_ref, col_ref, e_ref, c_ref, wide_ref, et_ref, ct_ref, e2_ref)

    rows, rank = a_ref.shape
    high = b_rows.shape[0]
    half = rows // 2
    value = (a_ref[...].astype(F32) * gain_ref[...]).astype(BF)
    scaled[...] = value
    turned = lax.dot_general(eye(high, half), b_ref[...], NT, preferred_element_type=F32)
    b_rows[...] = turned.astype(BF)
    value = value.astype(F32)
    upper = ring.y < dims[0] // 2
    rest = jnp.where(upper, value[half:], value[:half])
    if high > half:
        rest = jnp.concatenate([rest, jnp.zeros((high - half, rank), F32)], axis=0)
    give[...] = rest.astype(BF)
    entry.wait()
    exchange = remote(give, other, hsend, hrecv, ring.rows[dims[0] // 2 - 1])
    exchange.start()
    down.start(scaled, own_col.at[pl.ds(0, rows)], asems)
    up.start(b_rows, own_col.at[pl.ds(rows, high)], bsems)
    for load in loads:
        load.wait()
    work.tokens()
    exchange.wait_recv()
    both = jnp.where(upper, value[:half], value[half:]) + other[...].astype(F32)[:half]
    own_sec[...] = jnp.concatenate([both, turned[:half]], axis=0).astype(BF)
    first = Spread(ring, own_sec, sec_ref, first_sems)
    second = Spread(ring, own_col, col_ref, second_sems)
    third = Spread(ring, total_ref, gall_ref, third_sems)
    last = dims[1] // 2
    first.start()
    first.first()
    first.step(1)
    down.wait()
    up.wait()
    second.start()
    for k in range(2, last + 1):
        first.step(k)
        if k == 2:
            second.first()
        else:
            second.step(k - 2)
    if last < 2:
        second.first()
    first.landed()
    work.project(proj_ref)
    sent = []

    def push(*what):
        copy = remote(*what)
        copy.start()
        sent.append(copy)

    own = pltpu.make_async_copy(proj_ref, pall_ref.at[y0, x0], local_sem)
    own.start()
    push(proj_ref, pall_ref.at[y0, x0], across_send, across_recv, across)
    for j in range(1, width):
        push(proj_ref, pall_ref.at[y0, x0], xsend.at[0, j], xrecv.at[0, j], beside[j - 1])
    for k in range(max(1, last - 1), last + 1):
        second.step(k)
    second.landed()
    save = pltpu.make_async_copy(col_ref, col_out, save_col)
    save.start()
    work.gram(gram_ref)
    for j in range(1, count):
        push(gram_ref, landing.at[me], gsend.at[j], grecv.at[j], peers[j - 1])
    landing[me] = gram_ref[...]
    block = pall_ref.at[1 - y0, x0]
    remote(block, block, across_send, across_recv, across).wait_recv()
    for j in range(1, width):
        push(block, block, xsend.at[1, j], xrecv.at[1, j], beside[j - 1])
    for j in range(1, count):
        block = landing.at[lax.rem(me + count - j, count)]
        remote(block, block, gsend.at[j], grecv.at[j], peers[j - 1]).wait_recv()
    total = landing[0].astype(F32)
    for i in range(1, count):
        total = total + landing[i].astype(F32)
    total_ref[...] = total.astype(BF)
    third.start()
    third.first()
    for k in range(1, last + 1):
        third.step(k)
    for h in range(2):
        for j in range(1, width):
            landed = pall_ref.at[y0 if h == 0 else 1 - y0, lax.rem(x0 + width - j, width)]
            remote(landed, landed, xsend.at[h, j], xrecv.at[h, j], beside[j - 1]).wait_recv()
    third.finish()
    first.drain()
    second.drain()
    own.wait()
    save.wait()
    exchange.wait_send()
    for copy in sent:
        copy.wait_send()


def front(a, b, gain, embeds, cotangent, collective_id, make, dims=DP, secs=SEC, high=64):
    rows, rank = a.shape
    count = secs[0] * secs[1]
    tokens, width = embeds.shape
    dma = pltpu.SemaphoreType.DMA
    vmem = pl.BlockSpec(memory_space=pltpu.VMEM)
    anywhere = pl.BlockSpec(memory_space=pl.ANY)
    tall = rows + high
    shape = jax.ShapeDtypeStruct
    own_rows = (rows, high, high, high, rows, tall)
    return pl.pallas_call(
        functools.partial(front_kernel, dims, secs, make),
        out_shape=[
            shape(dims + (tall, rank), BF),
            shape(dims + (rank, rank), BF),
            shape(secs + (tokens, 3 * rank), BF),
            shape((width // count, tokens), BF),
            shape((width // count, tokens), BF),
            shape((tokens, 128), F32),
        ],
        in_specs=[vmem] * 3 + [anywhere] * 2,
        out_specs=[anywhere] * 3 + [vmem] * 3,
        scratch_shapes=[pltpu.VMEM((n, rank), BF) for n in own_rows]
        + [
            pltpu.VMEM(dims + (rows, rank), BF),
            pltpu.VMEM(dims + (tall, rank), BF),
            pltpu.VMEM((tokens, width), BF),
            pltpu.VMEM((tokens, width), BF),
            pltpu.VMEM((width, 2 * rank), BF),
            pltpu.VMEM((tokens, 3 * rank), BF),
            pltpu.VMEM((rank, rank), BF),
            pltpu.VMEM((count, rank, rank), BF),
            pltpu.VMEM((rank, rank), BF),
        ]
        + [dma, dma, dma, dma, dma, dma((3,)), dma((3,))]
        + [dma((count,)), dma((count,)), dma, dma, dma, dma((2, secs[1])), dma((2, secs[1]))]
        + ring_sems(dims) * 3,
        compiler_params=pltpu.CompilerParams(
            collective_id=collective_id, has_side_effects=True, vmem_limit_bytes=48 * 2**20
        ),
    )(a, b, gain, embeds, cotangent)


class Scatter:
    def __init__(self, ring, x_ref, rows, buffers, sems):
        self.ring, self.x, self.rows = ring, x_ref, rows
        self.from_core, self.moving, self.landing, self.rest, self.from_row = buffers
        self.sems = sems
        self.sent = []
        self.ready = set()
        self.totals = {}

    def push(self, *what):
        copy = remote(*what)
        copy.start()
        self.sent.append(copy)

    def start(self):
        ring = self.ring
        zs = ring.dims[1]
        csend, crecv = self.sems[:2]
        for offset in sorted(range(zs), key=lambda o: -min(o, zs - o)):
            z = lax.rem(ring.z + offset, zs)
            self.push(
                self.x.at[:, z, 1 - ring.c, self.rows],
                self.from_core.at[offset],
                csend.at[offset],
                crecv.at[offset],
                ring.sibling,
            )

    def need(self, offset):
        csend, crecv = self.sems[:2]
        if offset not in self.ready:
            self.ready.add(offset)
            block = self.from_core.at[offset]
            remote(block, block, csend.at[offset], crecv.at[offset], self.ring.sibling).wait_recv()

    def local_sum(self, offset, j):
        self.need(offset)
        ring = self.ring
        z = lax.rem(ring.z + offset, ring.dims[1])
        return self.x[j, z, ring.c, self.rows].astype(F32) + self.from_core[offset, j].astype(F32)

    def step(self, k):
        ring = self.ring
        ys, zs, _ = ring.dims
        zsend, zrecv = self.sems[2:4]
        for j in range(ys):
            for side in range(2):
                count = hops(zs, j, ys)[side]
                step = k - (zs // 2 - count)
                if step < 0:
                    continue
                reach = count - step
                offset = reach if side == 0 else (zs - reach) % zs
                got = 0.0
                if step:
                    spot = (side, j, step - 1)
                    block = self.landing.at[spot]
                    remote(block, block, zsend.at[spot], zrecv.at[spot], ring.sides[side]).wait_recv()
                    got = self.landing[spot].astype(F32)
                if reach:
                    spot = (side, j, step)
                    self.moving[spot] = (self.local_sum(offset, j) + got).astype(BF)
                    self.push(
                        self.moving.at[spot], self.landing.at[spot], zsend.at[spot], zrecv.at[spot], ring.sides[side]
                    )
                elif j not in self.totals:
                    self.totals[j] = self.local_sum(0, j) + got
                else:
                    self.rest[j] = (self.totals[j] + got).astype(BF)

    def rows_start(self):
        ring = self.ring
        ys = ring.dims[0]
        ysend, yrecv = self.sems[4:6]
        for i in range(1, ys):
            row = lax.rem(ring.y + i, ys)
            self.push(self.rest.at[row], self.from_row.at[i], ysend.at[i], yrecv.at[i], ring.rows[i - 1])

    def rows_finish(self):
        ring = self.ring
        ysend, yrecv = self.sems[4:6]
        own = self.rest[ring.y].astype(F32)
        for i in range(1, ring.dims[0]):
            block = self.from_row.at[i]
            remote(block, block, ysend.at[i], yrecv.at[i], ring.rows[i - 1]).wait_recv()
            own = own + self.from_row[i].astype(F32)
        return own

    def finish(self):
        for copy in self.sent:
            copy.wait_send()


def scatter_buffers(dims, rows, rank):
    ys, zs, _ = dims
    block = (rows, rank)
    shapes = [(zs, ys), (2, ys, zs // 2), (2, ys, zs // 2), (ys,), (ys,)]
    return [pltpu.VMEM(shape + block, BF) for shape in shapes]


def scatter_sems(dims):
    ys, zs, _ = dims
    dma = pltpu.SemaphoreType.DMA
    return [dma((zs,)), dma((zs,)), dma((2, ys, zs // 2)), dma((2, ys, zs // 2)), dma((ys,)), dma((ys,))]


def finish_kernel(dims, count, compute, inputs, *refs):
    given, refs = refs[:inputs], refs[inputs:]
    a_ref, gain_ref, ga_ref, gb_ref, gg_ref, ge_ref, x_ref, mine_low, got_low, mine_high = refs[:10]
    low_buffers, high_buffers = refs[10:15], refs[15:20]
    low_sems, high_sems = refs[20:26], refs[26:32]
    asems, gsend, grecv = refs[32:35]
    ring_part = refs[35:42]
    scratch = refs[42:]
    ring = Ring(dims)
    down, gather = swap_down(dims, count), Fan(ring, count, gb_ref, ring_part)
    me = lax.axis_index("section")
    peers = [{"section": lax.rem(me + j, count)} for j in range(1, count)]
    entry = Entry(ring.peers + peers, (down, gather))
    entry.count = entry.count + dims[0] - 1
    rows, rank = a_ref.shape
    high = mine_high.shape[0]
    upper = Scatter(ring, x_ref, pl.ds(rows, high), high_buffers, high_sems)
    lower = Scatter(ring, x_ref, pl.ds(0, rows), low_buffers, low_sems)
    work = compute(given, x_ref, ge_ref, scratch)
    work.ups()
    entry.wait()
    upper.start()
    upper.step(0)
    work.downs()
    lower.start()
    last = dims[1] // 2
    for k in range(1, last + 1):
        upper.step(k)
        if k > 1 or last == 1:
            lower.step(max(k - 2, 0))
    upper.rows_start()
    if last > 1:
        lower.step(last - 1)
    mine_high[...] = upper.rows_finish().astype(BF)
    gather.start_from(mine_high)
    lower.step(last)
    lower.rows_start()
    work.rest()
    mine_low[...] = lower.rows_finish().astype(BF)
    down.start(mine_low, got_low, asems)
    gather.first()
    down.wait()
    w = got_low[...].astype(F32)
    ga_ref[...] = w * gain_ref[...]
    prod = w * a_ref[...].astype(F32)
    if rank > rows:
        prod = jnp.concatenate([prod, jnp.zeros((rank - rows, rank), F32)], axis=0)
    line = lax.dot_general(
        jnp.ones((8, rank), F32), prod, NT, precision=lax.Precision.HIGHEST, preferred_element_type=F32
    )
    gg_ref[me] = line.astype(BF).astype(F32)
    sent = []
    for j in range(1, count):
        copy = remote(gg_ref.at[me], gg_ref.at[me], gsend.at[j], grecv.at[j], peers[j - 1])
        copy.start()
        sent.append(copy)
    for k in range(1, last + 1):
        gather.step(k)
    gather.finish()
    for j in range(1, count):
        block = gg_ref.at[lax.rem(me + count - j, count)]
        remote(block, block, gsend.at[j], grecv.at[j], peers[j - 1]).wait_recv()
    for copy in sent:
        copy.wait_send()
    upper.finish()
    lower.finish()


def finish(given, a, gain, ge_shape, compute, scratch, collective_id, dims=DP, count=CALLS, high=64):
    rows, rank = a.shape
    dma = pltpu.SemaphoreType.DMA
    vmem = pl.BlockSpec(memory_space=pltpu.VMEM)
    return pl.pallas_call(
        functools.partial(finish_kernel, dims, count, compute, len(given)),
        out_shape=[
            jax.ShapeDtypeStruct(a.shape, F32),
            jax.ShapeDtypeStruct(dims + (high, rank), BF),
            jax.ShapeDtypeStruct((count, 8, rank), F32),
            jax.ShapeDtypeStruct(ge_shape, BF),
        ],
        in_specs=[vmem] * (len(given) + 2),
        out_specs=[vmem, pl.BlockSpec(memory_space=pl.ANY), vmem, vmem],
        scratch_shapes=[pltpu.VMEM(dims + (rows + high, rank), BF)]
        + [pltpu.VMEM((n, rank), BF) for n in (rows, rows, high)]
        + scatter_buffers(dims, rows, rank)
        + scatter_buffers(dims, high, rank)
        + scatter_sems(dims) * 2
        + [dma((3,)), dma((count,)), dma((count,))]
        + ring_sems(dims)
        + scratch,
        compiler_params=pltpu.CompilerParams(
            collective_id=collective_id, has_side_effects=True, vmem_limit_bytes=48 * 2**20
        ),
    )(*given, a, gain)


class Solver:
    def __init__(self, given, x_ref, ge_ref, scratch):
        self.given, self.x, self.ge = given, x_ref, ge_ref
        self.r, self.v, self.w, self.hb, self.h, self.acc = scratch
        self.col = given[5]

    def down_rows(self, half, t):
        quarter = self.h.shape[1] // 4
        first = half * 4 * CALLS + t * 4
        return jnp.concatenate([self.col[first + j, :quarter] for j in range(4)], axis=0)

    def up_rows(self, t):
        quarter = self.h.shape[1] // 4
        eighth = quarter // 2
        pieces = [self.col[t * 8 + j, quarter:].astype(F32)[:eighth] for j in range(8)]
        return jnp.concatenate(pieces, axis=0).astype(BF)

    def put(self, index, rows, value):
        self.x[index // 16, index // 2 % 8, index % 2, rows] = value

    def ups(self):
        proj_ref, e2_ref, gram_ref, et_ref, ct_ref, _ = self.given
        r_ref, v_ref, w_ref, hb_ref, h_ref, acc_ref = self.r, self.v, self.w, self.hb, self.h, self.acc
        tokens, rank = r_ref.shape[1:]
        cols = et_ref.shape[0]
        scale = 1.0 / (2 * cols * CALLS)

        def gram(t, pos):
            return gram_ref[14 * t + pos if 2 * t < CALLS else 16 * (CALLS - 1 - t) + pos + 1]

        e2 = e2_ref[:, :1]
        h2 = e2
        invs = []
        for s in range(CALLS):
            pre = proj_ref[s, :, :rank].astype(F32)
            hb = proj_ref[s, :, rank : 2 * rank].astype(F32)
            for t in range(s):
                pre = pre + dot(r_ref[t], gram(t, 2 * s - 1))
                hb = hb + dot(r_ref[t], gram(t, 2 * s))
            inv = lax.rsqrt((e2 + h2) * scale + EPS)
            invs.append(inv)
            r = (pre * inv).astype(BF)
            r_ref[s] = r
            rn = dot(r, gram(s, 2 * s))
            h2 = h2 + jnp.sum(r.astype(F32) * (2.0 * hb + rn), axis=1, keepdims=True)
            hb_ref[s] = hb + rn

        lane = lax.broadcasted_iota(jnp.int32, (tokens, rank), 1)
        kap = jnp.zeros((tokens, 1), F32)
        kmat = jnp.zeros((tokens, rank), F32)
        for s in reversed(range(CALLS)):
            u = proj_ref[s, :, 2 * rank :].astype(F32) - kap * hb_ref[s]
            for t in range(s + 1, CALLS):
                u = u + dot_nt(v_ref[t], gram(s, 2 * t - 1)) + dot_nt(w_ref[t], gram(s, 2 * t))
            u = u.astype(BF).astype(F32)
            r = r_ref[s].astype(F32)
            inv = invs[s]
            q = jnp.sum(u * r, axis=1, keepdims=True) * scale
            k = inv * inv * q
            v_ref[s] = (inv * u).astype(BF)
            w_ref[s] = (-kap * r).astype(BF)
            kmat = jnp.where(lane == s, k, kmat)
            kap = kap + k

        unit = (
            lax.broadcasted_iota(jnp.int32, (CALLS, rank), 0) == lax.broadcasted_iota(jnp.int32, (CALLS, rank), 1)
        ).astype(F32)
        krows = lax.dot_general(unit, kmat, NT, precision=lax.Precision.HIGHEST, preferred_element_type=F32)

        quarter, eighth = cols // 4, cols // 8
        filler = jnp.zeros((64 - eighth, rank), F32)
        h_ref[0] = et_ref[...]
        for t in range(CALLS - 1):
            h_ref[t + 1] = (h_ref[t].astype(F32) + dot_nt(self.up_rows(t), r_ref[t])).astype(BF)
        back = ct_ref[...]
        for t in reversed(range(CALLS)):
            part = dot(back, r_ref[t])
            for j in range(8):
                piece = jnp.concatenate([part[j * eighth : (j + 1) * eighth], filler], axis=0)
                self.put(t * 8 + j, pl.ds(quarter, 64), piece.astype(BF))
            step = dot_nt(self.down_rows(0, t), v_ref[t]) - krows[t : t + 1] * h_ref[t].astype(F32)
            back = (back.astype(F32) + step).astype(BF)
        total = back.astype(F32) - jnp.sum(krows, axis=0, keepdims=True) * et_ref[...].astype(F32)
        acc_ref[...] = total

    def downs(self):
        et_ref = self.given[3]
        quarter = self.h.shape[1] // 4
        for t in range(CALLS):
            for half, source in ((0, self.h[t]), (1, et_ref[...])):
                value = dot(source, self.v[t]).astype(BF)
                for j in range(4):
                    index = half * 4 * CALLS + t * 4 + j
                    self.put(index, pl.ds(0, quarter), value[j * quarter : (j + 1) * quarter])

    def rest(self):
        for t in range(CALLS):
            self.acc[...] += dot_nt(self.down_rows(1, t), self.v[t])
        self.ge[...] = self.acc[...].astype(BF)


def per_device(embeds, cotangent, adapter_a, adapter_b, norm_gains):
    sec, dp = lax.axis_index("section"), lax.axis_index("dp")
    tokens, width = embeds.shape
    cols = width // CALLS
    a_own = adapter_a[0]
    quarter, rank = a_own.shape
    eighth = quarter // 2
    gain = jnp.where(sec % 2 == 0, norm_gains[0], norm_gains[1])
    gain_rows = lax.dynamic_slice_in_dim(gain, dp * quarter, quarter, 0)
    gain_rows = jnp.broadcast_to(gain_rows[:, None], (quarter, rank))
    col, gram, proj, et, ct, e2 = front(a_own, adapter_b[0], gain_rows, embeds, cotangent, 0, Front)
    col = col.reshape(64, quarter + 64, rank)
    gram = gram.reshape(64, rank, rank)
    proj = proj.reshape(CALLS, tokens, 3 * rank)

    scratch = [
        pltpu.VMEM((CALLS, tokens, rank), BF),
        pltpu.VMEM((CALLS, tokens, rank), BF),
        pltpu.VMEM((CALLS, tokens, rank), BF),
        pltpu.VMEM((CALLS, tokens, rank), F32),
        pltpu.VMEM((CALLS, cols, tokens), BF),
        pltpu.VMEM((cols, tokens), F32),
    ]
    grad_a, gb, gains, ge = finish(
        (proj, e2, gram, et, ct, col), a_own, gain_rows, (cols, tokens), Solver, scratch, 1
    )
    grad_gain = jnp.sum(gains.reshape(CALLS // 2, 2, 8, rank)[:, :, 0, :quarter], axis=0)
    grad_b = gb.reshape(64, 64, rank)[:, :eighth].reshape(width, rank)
    return (grad_a[None], grad_b.T.astype(F32)[None], grad_gain, ge.T)


def solution(mesh):
    in_specs = (
        P("dp", None),
        P("dp", None),
        P("section", "dp", None),
        P("section", None, "dp"),
        P(),
    )
    out_specs = (
        P("section", "dp", None),
        P("section", None, None),
        P(None, "dp"),
        P("dp", "section"),
    )
    return jax.shard_map(per_device, mesh=mesh, in_specs=in_specs, out_specs=out_specs, check_vma=False)
```

```python
import functools

import jax
import jax.numpy as jnp
from jax import lax
from jax.experimental import pallas as pl
from jax.experimental.pallas import tpu as pltpu
from jax.sharding import PartitionSpec as P

EPS = 1e-05
CALLS = 8
DP = (4, 8, 2)
SEC = (2, 4)
BF = jnp.bfloat16
F32 = jnp.float32
MESH = pl.DeviceIdType.MESH
NT = (((1,), (1,)), ((), ()))


class Entry:
    def __init__(self, peers, swaps=()):
        self.sem = pltpu.get_barrier_semaphore()
        self.count = len(peers)
        for peer in peers:
            pl.semaphore_signal(self.sem, inc=1, device_id=peer, device_id_type=MESH)
        for swap in swaps:
            swap.greet(self.sem)
            self.count = self.count + jnp.where(swap.stays, 0, 1)

    def wait(self):
        pl.semaphore_wait(self.sem, self.count)


def remote(src, dst, send, recv, peer):
    return pltpu.make_async_remote_copy(
        src_ref=src, dst_ref=dst, send_sem=send, recv_sem=recv, device_id=peer, device_id_type=MESH
    )


def hops(zs, stream, ys):
    long_way, short_way = zs // 2, zs - 1 - zs // 2
    return (long_way, short_way) if stream < ys // 2 else (short_way, long_way)


class Ring:
    def __init__(self, dims):
        self.dims = dims
        ys, zs, cs = dims
        me = lax.axis_index("dp")
        self.y, self.z, self.c = me // (zs * cs), lax.rem(me // cs, zs), lax.rem(me, cs)
        self.rows = [self.at(lax.rem(self.y + j, ys), self.z, self.c) for j in range(1, ys)]
        right, left = lax.rem(self.z + 1, zs), lax.rem(self.z + zs - 1, zs)
        self.sides = (self.at(self.y, right, self.c), self.at(self.y, left, self.c))
        self.sibling = self.at(self.y, self.z, 1 - self.c)
        self.peers = self.rows + list(self.sides) + [self.sibling]

    def at(self, y, z, c):
        _, zs, cs = self.dims
        return {"dp": (y * zs + z) * cs + c}


def ring_sems(dims):
    ys, zs, _ = dims
    dma = pltpu.SemaphoreType.DMA
    return [
        dma,
        dma((ys,)),
        dma((ys,)),
        dma((2, ys, zs // 2)),
        dma((2, ys, zs // 2)),
        dma((ys, zs)),
        dma((ys, zs)),
    ]


class Spread:
    def __init__(self, ring, src, out_ref, sems):
        self.ring, self.src, self.out, self.sems = ring, src, out_ref, sems
        self.sent = []
        self.own = None
        ys = ring.dims[0]
        self.lines = [lax.rem(ring.y + ys - j, ys) for j in range(ys)]

    def push(self, *what):
        copy = remote(*what)
        copy.start()
        self.sent.append(copy)

    def origin(self, side, k):
        zs = self.ring.dims[1]
        return lax.rem(self.ring.z + (zs - k if side == 0 else k), zs)

    def start(self):
        ring = self.ring
        local_sem, ysend, yrecv = self.sems[:3]
        block = self.out.at[ring.y, ring.z, ring.c]
        self.own = pltpu.make_async_copy(self.src, block, local_sem)
        self.own.start()
        for j in range(1, ring.dims[0]):
            self.push(self.src, block, ysend.at[j], yrecv.at[j], ring.rows[j - 1])

    def await_own(self):
        pass

    def relay(self, j, side, k):
        ring = self.ring
        zsend, zrecv = self.sems[3:5]
        block = self.out.at[self.lines[j], self.origin(side, k), ring.c]
        src = block if j or k or self.src is None else self.src
        self.push(src, block, zsend.at[side, j, k], zrecv.at[side, j, k], ring.sides[side])

    def share(self, j, z, index):
        ring = self.ring
        csend, crecv = self.sems[5:7]
        block = self.out.at[self.lines[j], z, ring.c]
        src = block if j or index or self.src is None else self.src
        self.push(src, block, csend.at[j, index], crecv.at[j, index], ring.sibling)

    def first(self):
        ring = self.ring
        ys, zs, _ = ring.dims
        ysend, yrecv = self.sems[1:3]
        for j in range(ys):
            if j:
                block = self.out.at[self.lines[j], ring.z, ring.c]
                remote(block, block, ysend.at[j], yrecv.at[j], ring.rows[j - 1]).wait_recv()
            else:
                self.await_own()
            for side in range(2):
                if hops(zs, j, ys)[side]:
                    self.relay(j, side, 0)
            self.share(j, ring.z, 0)

    def step(self, k):
        ring = self.ring
        ys, zs, _ = ring.dims
        zsend, zrecv = self.sems[3:5]
        for j in range(ys):
            for side in range(2):
                count = hops(zs, j, ys)[side]
                if k <= count:
                    z = self.origin(side, k)
                    block = self.out.at[self.lines[j], z, ring.c]
                    remote(
                        block, block, zsend.at[side, j, k - 1], zrecv.at[side, j, k - 1], ring.sides[side]
                    ).wait_recv()
                    if k < count:
                        self.relay(j, side, k)
                    self.share(j, z, zs - k if side == 0 else k)

    def landed(self):
        ring = self.ring
        ys, zs, _ = ring.dims
        csend, crecv = self.sems[5:7]
        for j in range(ys):
            for index in range(zs):
                block = self.out.at[self.lines[j], lax.rem(ring.z + index, zs), 1 - ring.c]
                remote(block, block, csend.at[j, index], crecv.at[j, index], ring.sibling).wait_recv()
        if self.own is not None:
            self.own.wait()

    def drain(self):
        for copy in self.sent:
            copy.wait_send()

    def finish(self):
        self.landed()
        self.drain()


class Fan(Spread):
    def __init__(self, ring, count, out_ref, sems):
        super().__init__(ring, None, out_ref, sems)
        ys, zs, cs = ring.dims
        step = ys * zs * cs // count
        sec, dp = lax.axis_index("section"), lax.axis_index("dp")
        self.call, slot = dp // step, sec * step + lax.rem(dp, step)
        self.stays = self.call == sec
        self.slot = (slot // (zs * cs), lax.rem(slot // cs, zs), lax.rem(slot, cs))
        self.targets, self.sources = [], []
        for i in range(ys):
            y = lax.rem(self.slot[0] + i, ys)
            self.targets.append({"section": self.call, **ring.at(y, *self.slot[1:])})
            place = (self.lines[i] * zs + ring.z) * cs + ring.c
            self.sources.append({"section": place // step, "dp": sec * step + lax.rem(place, step)})

    def greet(self, sem):
        for peer in self.sources[1:]:
            pl.semaphore_signal(sem, inc=1, device_id=peer, device_id_type=MESH)

        @pl.when(jnp.logical_not(self.stays))
        def _():
            pl.semaphore_signal(sem, inc=1, device_id=self.sources[0], device_id_type=MESH)

    def start_from(self, src):
        local_sem, ysend, yrecv = self.sems[:3]
        spot = self.out.at[self.slot]
        self.local = pltpu.make_async_copy(src, spot, local_sem)
        self.cross = remote(src, spot, ysend.at[0], yrecv.at[0], self.targets[0])

        @pl.when(self.stays)
        def _():
            self.local.start()

        @pl.when(jnp.logical_not(self.stays))
        def _():
            self.cross.start()

        for i in range(1, self.ring.dims[0]):
            self.push(src, spot, ysend.at[i], yrecv.at[i], self.targets[i])

    def await_own(self):
        ring = self.ring
        block = self.out.at[ring.y, ring.z, ring.c]
        ysend, yrecv = self.sems[1:3]

        @pl.when(self.stays)
        def _():
            self.local.wait()

        @pl.when(jnp.logical_not(self.stays))
        def _():
            remote(block, block, ysend.at[0], yrecv.at[0], self.targets[0]).wait_recv()

    def drain(self):
        super().drain()

        @pl.when(jnp.logical_not(self.stays))
        def _():
            self.cross.wait_send()


class Swap:
    def __init__(self, section, dp):
        self.peer = {"section": section, "dp": dp}
        self.stays = section == lax.axis_index("section")

    def greet(self, sem):
        @pl.when(jnp.logical_not(self.stays))
        def _():
            pl.semaphore_signal(sem, inc=1, device_id=self.peer, device_id_type=MESH)

    def start(self, src, dst, sems):
        self.local = pltpu.make_async_copy(src, dst, sems.at[0])
        self.remote = remote(src, dst, sems.at[1], sems.at[2], self.peer)

        @pl.when(self.stays)
        def _():
            self.local.start()

        @pl.when(jnp.logical_not(self.stays))
        def _():
            self.remote.start()

    def wait(self):
        @pl.when(self.stays)
        def _():
            self.local.wait()

        @pl.when(jnp.logical_not(self.stays))
        def _():
            self.remote.wait()


def swap_down(dims, count):
    size = dims[0] * dims[1] * dims[2]
    half, step = size // 2, size // 2 // count
    sec, dp = lax.axis_index("section"), lax.axis_index("dp")
    return Swap(lax.rem(dp, half) // step, dp // half * half + sec * step + lax.rem(dp, step))


def swap_up(dims, count):
    step = dims[0] * dims[1] * dims[2] // count
    sec, dp = lax.axis_index("section"), lax.axis_index("dp")
    return Swap(dp // step, sec * step + lax.rem(dp, step))


def dot(a, b):
    return jnp.dot(a, b, preferred_element_type=F32)


def dot_nt(a, b):
    return lax.dot_general(a, b, NT, preferred_element_type=F32)


def eye(rows, cols, shift=0, kind=BF):
    row = lax.broadcasted_iota(jnp.int32, (rows, cols), 0)
    col = lax.broadcasted_iota(jnp.int32, (rows, cols), 1)
    return (col == row + shift).astype(F32).astype(kind)


class Front:
    def __init__(self, sec_ref, col_ref, e_ref, c_ref, wide_ref, et_ref, ct_ref, e2_ref):
        self.sec, self.col, self.e, self.c, self.wide = sec_ref, col_ref, e_ref, c_ref, wide_ref
        self.et, self.ct, self.e2 = et_ref, ct_ref, e2_ref

    def tokens(self):
        cols, tokens = self.et.shape
        odd = 64 if cols % 128 else 0
        begin = lax.axis_index("section") * cols
        start = begin // 128 * 128
        window = pl.ds(pl.multiple_of(start, 128), cols + odd)
        pick = eye(cols, cols + odd, begin - start)
        self.et[...] = dot_nt(pick, self.e[:, window]).astype(BF)
        self.ct[...] = dot_nt(pick, self.c[:, window]).astype(BF)
        square = jnp.zeros((tokens, 128), F32)
        for i in range(self.e.shape[1] // 128):
            piece = self.e[:, i * 128 : (i + 1) * 128].astype(F32)
            square = square + piece * piece
        self.e2[...] = jnp.broadcast_to(jnp.sum(square, axis=1, keepdims=True), (tokens, 128))

    def project(self, out_ref):
        rows, rank = self.sec.shape[3:]
        half = rows // 2
        for i in range(32):
            y, z, c = i // 16, i // 2 % 8, i % 2
            low, high = self.sec[y, z, c].astype(F32), self.sec[y + 2, z, c].astype(F32)
            both = jnp.concatenate([low[:half], high[:half]], axis=0)
            self.wide[i * rows : (i + 1) * rows, :rank] = both.astype(BF)
            low, high = self.sec[i // 8, i % 8, 0].astype(F32), self.sec[i // 8, i % 8, 1].astype(F32)
            both = jnp.concatenate([low[half:], high[half:]], axis=0)
            self.wide[i * rows : (i + 1) * rows, rank:] = both.astype(BF)
        out_ref[:, : 2 * rank] = dot(self.e[...], self.wide[...]).astype(BF)
        out_ref[:, 2 * rank :] = dot(self.c[...], self.wide[:, rank:]).astype(BF)

    def block(self, index):
        return self.col[index // 16, lax.rem(index // 2, 8), lax.rem(index, 2)].astype(F32)

    def gram(self, out_ref):
        quarter = self.et.shape[0] // 4
        eighth = quarter // 2
        dp = lax.axis_index("dp")
        lead, spot = dp // 16, lax.rem(dp, 16)
        early = spot < 15 - 2 * lead
        row = jnp.where(early, lead, CALLS - 1 - lead)
        pos = jnp.where(early, 2 * lead + spot, spot - 1)
        other = (pos + 1) // 2
        even = lax.rem(pos, 2) == 0
        left = jnp.concatenate([self.block(row * 8 + j)[quarter:][:eighth] for j in range(8)], axis=0)
        ups = jnp.concatenate([self.block(other * 8 + j)[quarter:][:eighth] for j in range(8)], axis=0)
        downs = jnp.concatenate([self.block(other * 4 + j)[:quarter] for j in range(4)], axis=0)
        right = jnp.where(even, ups, downs)
        value = lax.dot_general(
            left.astype(BF), right.astype(BF), (((0,), (0,)), ((), ())), preferred_element_type=F32
        )
        out_ref[...] = value.astype(BF)


class Scatter:
    def __init__(self, ring, x_ref, rows, buffers, sems):
        self.ring, self.x, self.rows = ring, x_ref, rows
        self.from_core, self.moving, self.landing, self.rest, self.from_row = buffers
        self.sems = sems
        self.sent = []
        self.ready = set()
        self.totals = {}

    def push(self, *what):
        copy = remote(*what)
        copy.start()
        self.sent.append(copy)

    def start(self):
        ring = self.ring
        zs = ring.dims[1]
        csend, crecv = self.sems[:2]
        for offset in sorted(range(zs), key=lambda o: -min(o, zs - o)):
            z = lax.rem(ring.z + offset, zs)
            self.push(
                self.x.at[:, z, 1 - ring.c, self.rows],
                self.from_core.at[offset],
                csend.at[offset],
                crecv.at[offset],
                ring.sibling,
            )

    def need(self, offset):
        csend, crecv = self.sems[:2]
        if offset not in self.ready:
            self.ready.add(offset)
            block = self.from_core.at[offset]
            remote(block, block, csend.at[offset], crecv.at[offset], self.ring.sibling).wait_recv()

    def local_sum(self, offset, j):
        self.need(offset)
        ring = self.ring
        z = lax.rem(ring.z + offset, ring.dims[1])
        return self.x[j, z, ring.c, self.rows].astype(F32) + self.from_core[offset, j].astype(F32)

    def step(self, k):
        ring = self.ring
        ys, zs, _ = ring.dims
        zsend, zrecv = self.sems[2:4]
        for j in range(ys):
            for side in range(2):
                count = hops(zs, j, ys)[side]
                step = k - (zs // 2 - count)
                if step < 0:
                    continue
                reach = count - step
                offset = reach if side == 0 else (zs - reach) % zs
                got = 0.0
                if step:
                    spot = (side, j, step - 1)
                    block = self.landing.at[spot]
                    remote(block, block, zsend.at[spot], zrecv.at[spot], ring.sides[side]).wait_recv()
                    got = self.landing[spot].astype(F32)
                if reach:
                    spot = (side, j, step)
                    self.moving[spot] = (self.local_sum(offset, j) + got).astype(BF)
                    self.push(
                        self.moving.at[spot], self.landing.at[spot], zsend.at[spot], zrecv.at[spot], ring.sides[side]
                    )
                elif j not in self.totals:
                    self.totals[j] = self.local_sum(0, j) + got
                else:
                    self.rest[j] = (self.totals[j] + got).astype(BF)

    def rows_start(self):
        ring = self.ring
        ys = ring.dims[0]
        ysend, yrecv = self.sems[4:6]
        for i in range(1, ys):
            row = lax.rem(ring.y + i, ys)
            self.push(self.rest.at[row], self.from_row.at[i], ysend.at[i], yrecv.at[i], ring.rows[i - 1])

    def rows_finish(self):
        ring = self.ring
        ysend, yrecv = self.sems[4:6]
        own = self.rest[ring.y].astype(F32)
        for i in range(1, ring.dims[0]):
            block = self.from_row.at[i]
            remote(block, block, ysend.at[i], yrecv.at[i], ring.rows[i - 1]).wait_recv()
            own = own + self.from_row[i].astype(F32)
        return own

    def finish(self):
        for copy in self.sent:
            copy.wait_send()


def scatter_buffers(dims, rows, rank):
    ys, zs, _ = dims
    block = (rows, rank)
    shapes = [(zs, ys), (2, ys, zs // 2), (2, ys, zs // 2), (ys,), (ys,)]
    return [pltpu.VMEM(shape + block, BF) for shape in shapes]


def scatter_sems(dims):
    ys, zs, _ = dims
    dma = pltpu.SemaphoreType.DMA
    return [dma((zs,)), dma((zs,)), dma((2, ys, zs // 2)), dma((2, ys, zs // 2)), dma((ys,)), dma((ys,))]


def whole_kernel(dims, secs, make, compute, *refs):
    refs = list(refs)

    def take(n):
        got = refs[:n]
        del refs[:n]
        return got

    a_ref, b_ref, gain_ref, e_hbm, c_hbm = take(5)
    ga_ref, gb_ref, gg_ref, ge_ref = take(4)
    scaled, b_rows, give, other, own_sec, own_col = take(6)
    sec_ref, col_ref, e_ref, c_ref, wide_ref, proj_ref, gram_ref, landing, total_ref = take(9)
    gall_ref, pall_ref, et_ref, ct_ref, e2_ref = take(5)
    x_ref, mine_low, got_low, mine_high = take(4)
    low_buffers, high_buffers = take(5), take(5)
    load_e, load_c, hsend, hrecv, asems, bsems, csems = take(7)
    gsend, grecv, tsend, trecv, local_sem, across_send, across_recv, xsend, xrecv = take(9)
    first_sems, second_sems, third_sems, ring_part = take(7), take(7), take(7), take(7)
    low_sems, high_sems = take(6), take(6)
    scratch = refs
    ring = Ring(dims)
    count, width = secs[0] * secs[1], secs[1]
    me = lax.axis_index("section")
    y0, x0 = me // width, lax.rem(me, width)
    peers = [{"section": lax.rem(me + j, count)} for j in range(1, count)]
    across = {"section": (1 - y0) * width + x0}
    beside = [{"section": y0 * width + lax.rem(x0 + j, width)} for j in range(1, width)]
    down, up, back = swap_down(dims, count), swap_up(dims, count), swap_down(dims, count)
    gather = Fan(ring, count, gb_ref, ring_part)
    entry = Entry(ring.peers + peers, (down, up, gather))
    entry.count = entry.count + dims[0] - 1
    loads = [pltpu.make_async_copy(e_hbm, e_ref, load_e), pltpu.make_async_copy(c_hbm, c_ref, load_c)]
    for load in loads:
        load.start()
    work = make(sec_ref, col_ref, e_ref, c_ref, wide_ref, et_ref, ct_ref, e2_ref)

    rows, rank = a_ref.shape
    high = b_rows.shape[0]
    half = rows // 2
    value = (a_ref[...].astype(F32) * gain_ref[...]).astype(BF)
    scaled[...] = value
    turned = lax.dot_general(eye(high, half), b_ref[...], NT, preferred_element_type=F32)
    b_rows[...] = turned.astype(BF)
    value = value.astype(F32)
    upper = ring.y < dims[0] // 2
    rest = jnp.where(upper, value[half:], value[:half])
    if high > half:
        rest = jnp.concatenate([rest, jnp.zeros((high - half, rank), F32)], axis=0)
    give[...] = rest.astype(BF)
    entry.wait()
    exchange = remote(give, other, hsend, hrecv, ring.rows[dims[0] // 2 - 1])
    exchange.start()
    down.start(scaled, own_col.at[pl.ds(0, rows)], asems)
    up.start(b_rows, own_col.at[pl.ds(rows, high)], bsems)
    for load in loads:
        load.wait()
    work.tokens()
    exchange.wait_recv()
    both = jnp.where(upper, value[:half], value[half:]) + other[...].astype(F32)[:half]
    own_sec[...] = jnp.concatenate([both, turned[:half]], axis=0).astype(BF)
    first = Spread(ring, own_sec, sec_ref, first_sems)
    second = Spread(ring, own_col, col_ref, second_sems)
    third = Spread(ring, total_ref, gall_ref, third_sems)
    last = dims[1] // 2
    sent = []

    def push(*what):
        copy = remote(*what)
        copy.start()
        sent.append(copy)

    first.start()
    first.first()
    down.wait()
    up.wait()
    second.start()
    first.step(1)
    second.first()
    for k in range(1, last + 1):
        second.step(k)
        if k < last:
            first.step(k + 1)
    second.landed()
    work.gram(gram_ref)
    for j in range(1, count):
        push(gram_ref, landing.at[me], gsend.at[j], grecv.at[j], peers[j - 1])
    landing[me] = gram_ref[...]
    first.landed()
    work.project(proj_ref)
    own = pltpu.make_async_copy(proj_ref, pall_ref.at[y0, x0], local_sem)
    own.start()
    push(proj_ref, pall_ref.at[y0, x0], across_send, across_recv, across)
    for j in range(1, width):
        push(proj_ref, pall_ref.at[y0, x0], xsend.at[0, j], xrecv.at[0, j], beside[j - 1])
    for j in range(1, count):
        block = landing.at[lax.rem(me + count - j, count)]
        remote(block, block, gsend.at[j], grecv.at[j], peers[j - 1]).wait_recv()
    total = landing[0].astype(F32)
    for i in range(1, count):
        total = total + landing[i].astype(F32)
    total_ref[...] = total.astype(BF)
    third.start()
    third.first()
    third.step(1)
    block = pall_ref.at[1 - y0, x0]
    remote(block, block, across_send, across_recv, across).wait_recv()
    for j in range(1, width):
        push(block, block, xsend.at[1, j], xrecv.at[1, j], beside[j - 1])
    for k in range(2, last + 1):
        third.step(k)
    for h in range(2):
        for j in range(1, width):
            landed = pall_ref.at[y0 if h == 0 else 1 - y0, lax.rem(x0 + width - j, width)]
            remote(landed, landed, xsend.at[h, j], xrecv.at[h, j], beside[j - 1]).wait_recv()
    third.landed()
    own.wait()
    given = (pall_ref, e2_ref, gall_ref, et_ref, ct_ref, col_ref)
    raised = Scatter(ring, x_ref, pl.ds(rows, high), high_buffers, high_sems)
    lower = Scatter(ring, x_ref, pl.ds(0, rows), low_buffers, low_sems)
    solver = compute(given, x_ref, ge_ref, scratch)
    solver.ups()
    raised.start()
    raised.step(0)
    solver.downs()
    lower.start()
    last = dims[1] // 2
    for k in range(1, last + 1):
        raised.step(k)
        if k > 1 or last == 1:
            lower.step(max(k - 2, 0))
    raised.rows_start()
    if last > 1:
        lower.step(last - 1)
    mine_high[...] = raised.rows_finish().astype(BF)
    gather.start_from(mine_high)
    lower.step(last)
    lower.rows_start()
    solver.rest()
    mine_low[...] = lower.rows_finish().astype(BF)
    back.start(mine_low, got_low, csems)
    gather.first()
    back.wait()
    w = got_low[...].astype(F32)
    ga_ref[...] = w * gain_ref[...]
    prod = w * a_ref[...].astype(F32)
    if rank > rows:
        prod = jnp.concatenate([prod, jnp.zeros((rank - rows, rank), F32)], axis=0)
    line = lax.dot_general(
        jnp.ones((8, rank), F32), prod, NT, precision=lax.Precision.HIGHEST, preferred_element_type=F32
    )
    gg_ref[me] = line.astype(BF).astype(F32)
    for j in range(1, count):
        copy = remote(gg_ref.at[me], gg_ref.at[me], tsend.at[j], trecv.at[j], peers[j - 1])
        copy.start()
        sent.append(copy)
    for k in range(1, last + 1):
        gather.step(k)
    gather.finish()
    for j in range(1, count):
        block = gg_ref.at[lax.rem(me + count - j, count)]
        remote(block, block, tsend.at[j], trecv.at[j], peers[j - 1]).wait_recv()
    for copy in sent:
        copy.wait_send()
    raised.finish()
    lower.finish()
    first.drain()
    second.drain()
    third.drain()
    exchange.wait_send()


def whole(a, b, gain, embeds, cotangent, make, compute, scratch, dims=DP, secs=SEC, high=64):
    rows, rank = a.shape
    count = secs[0] * secs[1]
    tokens, width = embeds.shape
    cols = width // count
    dma = pltpu.SemaphoreType.DMA
    vmem = pl.BlockSpec(memory_space=pltpu.VMEM)
    anywhere = pl.BlockSpec(memory_space=pl.ANY)
    tall = rows + high
    shape = jax.ShapeDtypeStruct

    def buffer(*size, kind=BF):
        return pltpu.VMEM(size, kind)

    return pl.pallas_call(
        functools.partial(whole_kernel, dims, secs, make, compute),
        out_shape=[
            shape(a.shape, F32),
            shape(dims + (high, rank), BF),
            shape((count, 8, rank), F32),
            shape((cols, tokens), BF),
        ],
        in_specs=[vmem] * 3 + [anywhere] * 2,
        out_specs=[vmem, anywhere, vmem, vmem],
        scratch_shapes=[buffer(n, rank) for n in (rows, high, high, high, rows, tall)]
        + [
            buffer(*dims, rows, rank),
            buffer(*dims, tall, rank),
            buffer(tokens, width),
            buffer(tokens, width),
            buffer(width, 2 * rank),
            buffer(tokens, 3 * rank),
            buffer(rank, rank),
            buffer(count, rank, rank),
            buffer(rank, rank),
            buffer(*dims, rank, rank),
            buffer(*secs, tokens, 3 * rank),
            buffer(cols, tokens),
            buffer(cols, tokens),
            buffer(tokens, 128, kind=F32),
            buffer(*dims, tall, rank),
        ]
        + [buffer(n, rank) for n in (rows, rows, high)]
        + scatter_buffers(dims, rows, rank)
        + scatter_buffers(dims, high, rank)
        + [dma] * 4
        + [dma((3,))] * 3
        + [dma((count,))] * 4
        + [dma] * 3
        + [dma((2, secs[1]))] * 2
        + ring_sems(dims) * 4
        + scatter_sems(dims) * 2
        + scratch,
        compiler_params=pltpu.CompilerParams(
            collective_id=0, has_side_effects=True, vmem_limit_bytes=58 * 2**20
        ),
    )(a, b, gain, embeds, cotangent)


def dp_spot(index):
    return index // 16, index // 2 % 8, index % 2


class Solver:
    def __init__(self, given, x_ref, ge_ref, scratch):
        self.given, self.x, self.ge = given, x_ref, ge_ref
        self.r, self.v, self.w, self.hb, self.h, self.acc = scratch
        self.col = given[5]

    def down_rows(self, half, t):
        quarter = self.h.shape[1] // 4
        first = half * 4 * CALLS + t * 4
        return jnp.concatenate([self.col[dp_spot(first + j)][:quarter] for j in range(4)], axis=0)

    def up_rows(self, t):
        quarter = self.h.shape[1] // 4
        eighth = quarter // 2
        pieces = [self.col[dp_spot(t * 8 + j)][quarter:].astype(F32)[:eighth] for j in range(8)]
        return jnp.concatenate(pieces, axis=0).astype(BF)

    def put(self, index, rows, value):
        self.x[(*dp_spot(index), rows)] = value

    def ups(self):
        proj_ref, e2_ref, gram_ref, et_ref, ct_ref, _ = self.given
        r_ref, v_ref, w_ref, hb_ref, h_ref, acc_ref = self.r, self.v, self.w, self.hb, self.h, self.acc
        tokens, rank = r_ref.shape[1:]
        cols = et_ref.shape[0]
        scale = 1.0 / (2 * cols * CALLS)

        def gram(t, pos):
            return gram_ref[dp_spot(14 * t + pos if 2 * t < CALLS else 16 * (CALLS - 1 - t) + pos + 1)]

        e2 = e2_ref[:, :1]
        h2 = e2
        invs = []
        for s in range(CALLS):
            pre = proj_ref[s // 4, s % 4, :, :rank].astype(F32)
            hb = proj_ref[s // 4, s % 4, :, rank : 2 * rank].astype(F32)
            for t in range(s):
                pre = pre + dot(r_ref[t], gram(t, 2 * s - 1))
                hb = hb + dot(r_ref[t], gram(t, 2 * s))
            inv = lax.rsqrt((e2 + h2) * scale + EPS)
            invs.append(inv)
            r = (pre * inv).astype(BF)
            r_ref[s] = r
            rn = dot(r, gram(s, 2 * s))
            h2 = h2 + jnp.sum(r.astype(F32) * (2.0 * hb + rn), axis=1, keepdims=True)
            hb_ref[s] = hb + rn

        lane = lax.broadcasted_iota(jnp.int32, (tokens, rank), 1)
        kap = jnp.zeros((tokens, 1), F32)
        kmat = jnp.zeros((tokens, rank), F32)
        for s in reversed(range(CALLS)):
            u = proj_ref[s // 4, s % 4, :, 2 * rank :].astype(F32) - kap * hb_ref[s]
            for t in range(s + 1, CALLS):
                u = u + dot_nt(v_ref[t], gram(s, 2 * t - 1)) + dot_nt(w_ref[t], gram(s, 2 * t))
            u = u.astype(BF).astype(F32)
            r = r_ref[s].astype(F32)
            inv = invs[s]
            q = jnp.sum(u * r, axis=1, keepdims=True) * scale
            k = inv * inv * q
            v_ref[s] = (inv * u).astype(BF)
            w_ref[s] = (-kap * r).astype(BF)
            kmat = jnp.where(lane == s, k, kmat)
            kap = kap + k

        unit = (
            lax.broadcasted_iota(jnp.int32, (CALLS, rank), 0) == lax.broadcasted_iota(jnp.int32, (CALLS, rank), 1)
        ).astype(F32)
        krows = lax.dot_general(unit, kmat, NT, precision=lax.Precision.HIGHEST, preferred_element_type=F32)

        quarter, eighth = cols // 4, cols // 8
        filler = jnp.zeros((64 - eighth, rank), F32)
        h_ref[0] = et_ref[...]
        for t in range(CALLS - 1):
            h_ref[t + 1] = (h_ref[t].astype(F32) + dot_nt(self.up_rows(t), r_ref[t])).astype(BF)
        back = ct_ref[...]
        for t in reversed(range(CALLS)):
            part = dot(back, r_ref[t])
            for j in range(8):
                piece = jnp.concatenate([part[j * eighth : (j + 1) * eighth], filler], axis=0)
                self.put(t * 8 + j, pl.ds(quarter, 64), piece.astype(BF))
            step = dot_nt(self.down_rows(0, t), v_ref[t]) - krows[t : t + 1] * h_ref[t].astype(F32)
            back = (back.astype(F32) + step).astype(BF)
        total = back.astype(F32) - jnp.sum(krows, axis=0, keepdims=True) * et_ref[...].astype(F32)
        acc_ref[...] = total

    def downs(self):
        et_ref = self.given[3]
        quarter = self.h.shape[1] // 4
        for t in range(CALLS):
            for half, source in ((0, self.h[t]), (1, et_ref[...])):
                value = dot(source, self.v[t]).astype(BF)
                for j in range(4):
                    index = half * 4 * CALLS + t * 4 + j
                    self.put(index, pl.ds(0, quarter), value[j * quarter : (j + 1) * quarter])

    def rest(self):
        for t in range(CALLS):
            self.acc[...] += dot_nt(self.down_rows(1, t), self.v[t])
        self.ge[...] = self.acc[...].astype(BF)


def per_device(embeds, cotangent, adapter_a, adapter_b, norm_gains):
    sec, dp = lax.axis_index("section"), lax.axis_index("dp")
    tokens, width = embeds.shape
    cols = width // CALLS
    a_own = adapter_a[0]
    quarter, rank = a_own.shape
    eighth = quarter // 2
    gain = jnp.where(sec % 2 == 0, norm_gains[0], norm_gains[1])
    gain_rows = lax.dynamic_slice_in_dim(gain, dp * quarter, quarter, 0)
    gain_rows = jnp.broadcast_to(gain_rows[:, None], (quarter, rank))
    scratch = [
        pltpu.VMEM((CALLS, tokens, rank), BF),
        pltpu.VMEM((CALLS, tokens, rank), BF),
        pltpu.VMEM((CALLS, tokens, rank), BF),
        pltpu.VMEM((CALLS, tokens, rank), F32),
        pltpu.VMEM((CALLS, cols, tokens), BF),
        pltpu.VMEM((cols, tokens), F32),
    ]
    grad_a, gb, gains, ge = whole(
        a_own, adapter_b[0], gain_rows, embeds, cotangent, Front, Solver, scratch
    )
    grad_gain = jnp.sum(gains.reshape(CALLS // 2, 2, 8, rank)[:, :, 0, :quarter], axis=0)
    grad_b = gb.reshape(64, 64, rank)[:, :eighth].reshape(width, rank)
    return (grad_a[None], grad_b.T.astype(F32)[None], grad_gain, ge.T)


def solution(mesh):
    in_specs = (
        P("dp", None),
        P("dp", None),
        P("section", "dp", None),
        P("section", None, "dp"),
        P(),
    )
    out_specs = (
        P("section", "dp", None),
        P("section", None, None),
        P(None, "dp"),
        P("dp", "section"),
    )
    return jax.shard_map(per_device, mesh=mesh, in_specs=in_specs, out_specs=out_specs, check_vma=False)
```

```python
import functools

import jax
import jax.numpy as jnp
from jax import lax
from jax.experimental import pallas as pl
from jax.experimental.pallas import tpu as pltpu
from jax.sharding import PartitionSpec as P

EPS = 1e-05
CALLS = 8
DP = (4, 8, 2)
SEC = (2, 4)
BF = jnp.bfloat16
F32 = jnp.float32
MESH = pl.DeviceIdType.MESH
NT = (((1,), (1,)), ((), ()))


class Entry:
    def __init__(self, peers, swaps=()):
        self.sem = pltpu.get_barrier_semaphore()
        self.count = len(peers)
        for peer in peers:
            pl.semaphore_signal(self.sem, inc=1, device_id=peer, device_id_type=MESH)
        for swap in swaps:
            swap.greet(self.sem)
            self.count = self.count + jnp.where(swap.stays, 0, 1)

    def wait(self):
        pl.semaphore_wait(self.sem, self.count)


def remote(src, dst, send, recv, peer):
    return pltpu.make_async_remote_copy(
        src_ref=src, dst_ref=dst, send_sem=send, recv_sem=recv, device_id=peer, device_id_type=MESH
    )


def hops(zs, stream, ys):
    long_way, short_way = zs // 2, zs - 1 - zs // 2
    return (long_way, short_way) if stream < ys // 2 else (short_way, long_way)


class Ring:
    def __init__(self, dims):
        self.dims = dims
        ys, zs, cs = dims
        me = lax.axis_index("dp")
        self.y, self.z, self.c = me // (zs * cs), lax.rem(me // cs, zs), lax.rem(me, cs)
        self.rows = [self.at(lax.rem(self.y + j, ys), self.z, self.c) for j in range(1, ys)]
        right, left = lax.rem(self.z + 1, zs), lax.rem(self.z + zs - 1, zs)
        self.sides = (self.at(self.y, right, self.c), self.at(self.y, left, self.c))
        self.sibling = self.at(self.y, self.z, 1 - self.c)
        self.peers = self.rows + list(self.sides) + [self.sibling]

    def at(self, y, z, c):
        _, zs, cs = self.dims
        return {"dp": (y * zs + z) * cs + c}


def ring_sems(dims):
    ys, zs, _ = dims
    dma = pltpu.SemaphoreType.DMA
    return [
        dma,
        dma((ys,)),
        dma((ys,)),
        dma((2, ys, zs // 2)),
        dma((2, ys, zs // 2)),
        dma((ys, zs)),
        dma((ys, zs)),
    ]


class Spread:
    def __init__(self, ring, src, out_ref, sems):
        self.ring, self.src, self.out, self.sems = ring, src, out_ref, sems
        self.sent = []
        self.own = None
        ys = ring.dims[0]
        self.lines = [lax.rem(ring.y + ys - j, ys) for j in range(ys)]

    def push(self, *what):
        copy = remote(*what)
        copy.start()
        self.sent.append(copy)

    def origin(self, side, k):
        zs = self.ring.dims[1]
        return lax.rem(self.ring.z + (zs - k if side == 0 else k), zs)

    def start(self):
        ring = self.ring
        local_sem, ysend, yrecv = self.sems[:3]
        block = self.out.at[ring.y, ring.z, ring.c]
        self.own = pltpu.make_async_copy(self.src, block, local_sem)
        self.own.start()
        for j in range(1, ring.dims[0]):
            self.push(self.src, block, ysend.at[j], yrecv.at[j], ring.rows[j - 1])

    def relay(self, j, side, k):
        ring = self.ring
        zsend, zrecv = self.sems[3:5]
        block = self.out.at[self.lines[j], self.origin(side, k), ring.c]
        src = block if j or k or self.src is None else self.src
        self.push(src, block, zsend.at[side, j, k], zrecv.at[side, j, k], ring.sides[side])

    def share(self, j, z, index):
        ring = self.ring
        csend, crecv = self.sems[5:7]
        block = self.out.at[self.lines[j], z, ring.c]
        src = block if j or index or self.src is None else self.src
        self.push(src, block, csend.at[j, index], crecv.at[j, index], ring.sibling)

    def first(self):
        ring = self.ring
        ys, zs, _ = ring.dims
        ysend, yrecv = self.sems[1:3]
        for j in range(ys):
            if j:
                block = self.out.at[self.lines[j], ring.z, ring.c]
                remote(block, block, ysend.at[j], yrecv.at[j], ring.rows[j - 1]).wait_recv()
            for side in range(2):
                if hops(zs, j, ys)[side]:
                    self.relay(j, side, 0)
            self.share(j, ring.z, 0)

    def step(self, k):
        ring = self.ring
        ys, zs, _ = ring.dims
        zsend, zrecv = self.sems[3:5]
        for j in range(ys):
            for side in range(2):
                count = hops(zs, j, ys)[side]
                if k <= count:
                    z = self.origin(side, k)
                    block = self.out.at[self.lines[j], z, ring.c]
                    remote(
                        block, block, zsend.at[side, j, k - 1], zrecv.at[side, j, k - 1], ring.sides[side]
                    ).wait_recv()
                    if k < count:
                        self.relay(j, side, k)
                    self.share(j, z, zs - k if side == 0 else k)

    def landed(self):
        ring = self.ring
        ys, zs, _ = ring.dims
        csend, crecv = self.sems[5:7]
        for j in range(ys):
            for index in range(zs):
                block = self.out.at[self.lines[j], lax.rem(ring.z + index, zs), 1 - ring.c]
                remote(block, block, csend.at[j, index], crecv.at[j, index], ring.sibling).wait_recv()
        if self.own is not None:
            self.own.wait()

    def drain(self):
        for copy in self.sent:
            copy.wait_send()

    def finish(self):
        self.landed()
        self.drain()


class Fan(Spread):
    def __init__(self, ring, count, out_ref, sems):
        super().__init__(ring, None, out_ref, sems)
        ys, zs, cs = ring.dims
        step = ys * zs * cs // count
        sec, dp = lax.axis_index("section"), lax.axis_index("dp")
        self.call, slot = dp // step, sec * step + lax.rem(dp, step)
        self.stays = self.call == sec
        self.slot = (slot // (zs * cs), lax.rem(slot // cs, zs), lax.rem(slot, cs))
        self.targets, self.sources = [], []
        self.far = [ring.at(ring.y, lax.rem(ring.z + o, zs), ring.c) for o in range(2, zs - 1)]
        for i in range(ys):
            y = lax.rem(self.slot[0] + i, ys)
            self.targets.append({"section": self.call, **ring.at(y, *self.slot[1:])})
            place = (self.lines[i] * zs + ring.z) * cs + ring.c
            self.sources.append({"section": place // step, "dp": sec * step + lax.rem(place, step)})

    def greet(self, sem):
        for peer in self.sources[1:] + self.far:
            pl.semaphore_signal(sem, inc=1, device_id=peer, device_id_type=MESH)

        @pl.when(jnp.logical_not(self.stays))
        def _():
            pl.semaphore_signal(sem, inc=1, device_id=self.sources[0], device_id_type=MESH)

    def start_from(self, src):
        local_sem, ysend, yrecv = self.sems[:3]
        spot = self.out.at[self.slot]
        self.local = pltpu.make_async_copy(src, spot, local_sem)
        self.cross = remote(src, spot, ysend.at[0], yrecv.at[0], self.targets[0])

        @pl.when(self.stays)
        def _():
            self.local.start()

        @pl.when(jnp.logical_not(self.stays))
        def _():
            self.cross.start()

        for i in range(1, self.ring.dims[0]):
            self.push(src, spot, ysend.at[i], yrecv.at[i], self.targets[i])

    def spots(self):
        zs = self.ring.dims[1]
        half = zs // 2
        near_first = sorted(range(1, zs), key=lambda o: min(o, zs - o))
        return [(o, (0, o - 1) if o <= half else (1, o - half - 1)) for o in near_first]

    def first(self):
        ring = self.ring
        ys, zs, _ = ring.dims
        ysend, yrecv, zsend, zrecv = self.sems[1:5]
        for j in range(ys):
            block = self.out.at[self.lines[j], ring.z, ring.c]
            if j:
                remote(block, block, ysend.at[j], yrecv.at[j], ring.rows[j - 1]).wait_recv()
            else:
                self.await_own()
            for o, (side, k) in reversed(self.spots()):
                peer = ring.at(ring.y, lax.rem(ring.z + o, zs), ring.c)
                self.push(block, block, zsend.at[side, j, k], zrecv.at[side, j, k], peer)
            self.share(j, ring.z, 0)

    def collect(self):
        ring = self.ring
        ys, zs, _ = ring.dims
        zsend, zrecv = self.sems[3:5]
        for o, (side, k) in self.spots():
            for j in range(ys):
                z = lax.rem(ring.z + zs - o, zs)
                block = self.out.at[self.lines[j], z, ring.c]
                remote(block, block, zsend.at[side, j, k], zrecv.at[side, j, k], ring.sides[0]).wait_recv()
                self.share(j, z, zs - o)

    def await_own(self):
        ring = self.ring
        block = self.out.at[ring.y, ring.z, ring.c]
        ysend, yrecv = self.sems[1:3]

        @pl.when(self.stays)
        def _():
            self.local.wait()

        @pl.when(jnp.logical_not(self.stays))
        def _():
            remote(block, block, ysend.at[0], yrecv.at[0], self.targets[0]).wait_recv()

    def drain(self):
        super().drain()

        @pl.when(jnp.logical_not(self.stays))
        def _():
            self.cross.wait_send()


class Swap:
    def __init__(self, section, dp):
        self.peer = {"section": section, "dp": dp}
        self.stays = section == lax.axis_index("section")

    def greet(self, sem):
        @pl.when(jnp.logical_not(self.stays))
        def _():
            pl.semaphore_signal(sem, inc=1, device_id=self.peer, device_id_type=MESH)

    def start(self, src, dst, sems):
        self.local = pltpu.make_async_copy(src, dst, sems.at[0])
        self.remote = remote(src, dst, sems.at[1], sems.at[2], self.peer)

        @pl.when(self.stays)
        def _():
            self.local.start()

        @pl.when(jnp.logical_not(self.stays))
        def _():
            self.remote.start()

    def wait(self):
        @pl.when(self.stays)
        def _():
            self.local.wait()

        @pl.when(jnp.logical_not(self.stays))
        def _():
            self.remote.wait()


def swap_down(dims, count):
    size = dims[0] * dims[1] * dims[2]
    half, step = size // 2, size // 2 // count
    sec, dp = lax.axis_index("section"), lax.axis_index("dp")
    return Swap(lax.rem(dp, half) // step, dp // half * half + sec * step + lax.rem(dp, step))


def swap_up(dims, count):
    step = dims[0] * dims[1] * dims[2] // count
    sec, dp = lax.axis_index("section"), lax.axis_index("dp")
    return Swap(dp // step, sec * step + lax.rem(dp, step))


def dot(a, b):
    return jnp.dot(a, b, preferred_element_type=F32)


def dot_nt(a, b):
    return lax.dot_general(a, b, NT, preferred_element_type=F32)


def eye(rows, cols, shift=0, kind=BF):
    row = lax.broadcasted_iota(jnp.int32, (rows, cols), 0)
    col = lax.broadcasted_iota(jnp.int32, (rows, cols), 1)
    return (col == row + shift).astype(F32).astype(kind)


class Front:
    def __init__(self, sec_ref, col_ref, e_ref, c_ref, wide_ref, et_ref, ct_ref, e2_ref):
        self.sec, self.col, self.e, self.c, self.wide = sec_ref, col_ref, e_ref, c_ref, wide_ref
        self.et, self.ct, self.e2 = et_ref, ct_ref, e2_ref

    def tokens(self):
        cols, tokens = self.et.shape
        odd = 64 if cols % 128 else 0
        begin = lax.axis_index("section") * cols
        start = begin // 128 * 128
        window = pl.ds(pl.multiple_of(start, 128), cols + odd)
        pick = eye(cols, cols + odd, begin - start)
        self.et[...] = dot_nt(pick, self.e[:, window]).astype(BF)
        self.ct[...] = dot_nt(pick, self.c[:, window]).astype(BF)
        square = jnp.zeros((tokens, 128), F32)
        for i in range(self.e.shape[1] // 128):
            piece = self.e[:, i * 128 : (i + 1) * 128].astype(F32)
            square = square + piece * piece
        self.e2[...] = jnp.broadcast_to(jnp.sum(square, axis=1, keepdims=True), (tokens, 128))

    def project(self, out_ref):
        rows, rank = self.sec.shape[3:]
        half = rows // 2
        for i in range(32):
            y, z, c = i // 16, i // 2 % 8, i % 2
            low, high = self.sec[y, z, c].astype(F32), self.sec[y + 2, z, c].astype(F32)
            both = jnp.concatenate([low[:half], high[:half]], axis=0)
            self.wide[i * rows : (i + 1) * rows, :rank] = both.astype(BF)
            low, high = self.sec[i // 8, i % 8, 0].astype(F32), self.sec[i // 8, i % 8, 1].astype(F32)
            both = jnp.concatenate([low[half:], high[half:]], axis=0)
            self.wide[i * rows : (i + 1) * rows, rank:] = both.astype(BF)
        out_ref[:, : 2 * rank] = dot(self.e[...], self.wide[...]).astype(BF)
        out_ref[:, 2 * rank :] = dot(self.c[...], self.wide[:, rank:]).astype(BF)

    def block(self, index):
        return self.col[index // 16, lax.rem(index // 2, 8), lax.rem(index, 2)].astype(F32)

    def gram(self, out_ref):
        quarter = self.et.shape[0] // 4
        eighth = quarter // 2
        dp = lax.axis_index("dp")
        lead, spot = dp // 16, lax.rem(dp, 16)
        early = spot < 15 - 2 * lead
        row = jnp.where(early, lead, CALLS - 1 - lead)
        pos = jnp.where(early, 2 * lead + spot, spot - 1)
        other = (pos + 1) // 2
        even = lax.rem(pos, 2) == 0
        left = jnp.concatenate([self.block(row * 8 + j)[quarter:][:eighth] for j in range(8)], axis=0)
        ups = jnp.concatenate([self.block(other * 8 + j)[quarter:][:eighth] for j in range(8)], axis=0)
        downs = jnp.concatenate([self.block(other * 4 + j)[:quarter] for j in range(4)], axis=0)
        right = jnp.where(even, ups, downs)
        value = lax.dot_general(
            left.astype(BF), right.astype(BF), (((0,), (0,)), ((), ())), preferred_element_type=F32
        )
        out_ref[...] = value.astype(BF)


class Scatter:
    def __init__(self, ring, x_ref, rows, buffers, sems):
        self.ring, self.x, self.rows = ring, x_ref, rows
        self.from_core, self.moving, self.landing, self.rest, self.from_row = buffers
        self.sems = sems
        self.sent = []
        self.ready = set()
        self.totals = {}

    def push(self, *what):
        copy = remote(*what)
        copy.start()
        self.sent.append(copy)

    def start(self):
        ring = self.ring
        zs = ring.dims[1]
        csend, crecv = self.sems[:2]
        for offset in sorted(range(zs), key=lambda o: -min(o, zs - o)):
            z = lax.rem(ring.z + offset, zs)
            self.push(
                self.x.at[:, z, 1 - ring.c, self.rows],
                self.from_core.at[offset],
                csend.at[offset],
                crecv.at[offset],
                ring.sibling,
            )

    def need(self, offset):
        csend, crecv = self.sems[:2]
        if offset not in self.ready:
            self.ready.add(offset)
            block = self.from_core.at[offset]
            remote(block, block, csend.at[offset], crecv.at[offset], self.ring.sibling).wait_recv()

    def local_sum(self, offset, j):
        self.need(offset)
        ring = self.ring
        z = lax.rem(ring.z + offset, ring.dims[1])
        return self.x[j, z, ring.c, self.rows].astype(F32) + self.from_core[offset, j].astype(F32)

    def step(self, k):
        ring = self.ring
        ys, zs, _ = ring.dims
        zsend, zrecv = self.sems[2:4]
        for j in range(ys):
            for side in range(2):
                count = hops(zs, j, ys)[side]
                step = k - (zs // 2 - count)
                if step < 0:
                    continue
                reach = count - step
                offset = reach if side == 0 else (zs - reach) % zs
                got = 0.0
                if step:
                    spot = (side, j, step - 1)
                    block = self.landing.at[spot]
                    remote(block, block, zsend.at[spot], zrecv.at[spot], ring.sides[side]).wait_recv()
                    got = self.landing[spot].astype(F32)
                if reach:
                    spot = (side, j, step)
                    self.moving[spot] = (self.local_sum(offset, j) + got).astype(BF)
                    self.push(
                        self.moving.at[spot], self.landing.at[spot], zsend.at[spot], zrecv.at[spot], ring.sides[side]
                    )
                elif j not in self.totals:
                    self.totals[j] = self.local_sum(0, j) + got
                else:
                    self.rest[j] = (self.totals[j] + got).astype(BF)

    def rows_start(self):
        ring = self.ring
        ys = ring.dims[0]
        ysend, yrecv = self.sems[4:6]
        for i in range(1, ys):
            row = lax.rem(ring.y + i, ys)
            self.push(self.rest.at[row], self.from_row.at[i], ysend.at[i], yrecv.at[i], ring.rows[i - 1])

    def rows_finish(self):
        ring = self.ring
        ysend, yrecv = self.sems[4:6]
        own = self.rest[ring.y].astype(F32)
        for i in range(1, ring.dims[0]):
            block = self.from_row.at[i]
            remote(block, block, ysend.at[i], yrecv.at[i], ring.rows[i - 1]).wait_recv()
            own = own + self.from_row[i].astype(F32)
        return own

    def finish(self):
        for copy in self.sent:
            copy.wait_send()


def scatter_buffers(dims, rows, rank):
    ys, zs, _ = dims
    block = (rows, rank)
    shapes = [(zs, ys), (2, ys, zs // 2), (2, ys, zs // 2), (ys,), (ys,)]
    return [pltpu.VMEM(shape + block, BF) for shape in shapes]


def scatter_sems(dims):
    ys, zs, _ = dims
    dma = pltpu.SemaphoreType.DMA
    return [dma((zs,)), dma((zs,)), dma((2, ys, zs // 2)), dma((2, ys, zs // 2)), dma((ys,)), dma((ys,))]


def whole_kernel(dims, secs, make, compute, *refs):
    refs = list(refs)

    def take(n):
        got = refs[:n]
        del refs[:n]
        return got

    a_ref, b_ref, gain_ref, e_hbm, c_hbm = take(5)
    ga_ref, up_ref, gain_out, ge_ref = take(4)
    scaled, b_rows, give, other, own_sec, own_col = take(6)
    sec_ref, col_ref, e_ref, c_ref, wide_ref, proj_ref, gram_ref, landing, total_ref = take(9)
    gall_ref, pall_ref, et_ref, ct_ref, e2_ref = take(5)
    gb_ref, gg_ref = take(2)
    x_ref, mine_low, got_low, mine_high = take(4)
    low_buffers, high_buffers = take(5), take(5)
    load_e, load_c, hsend, hrecv, asems, bsems, csems = take(7)
    gsend, grecv, tsend, trecv, local_sem, across_send, across_recv, xsend, xrecv = take(9)
    first_sems, second_sems, third_sems, ring_part = take(7), take(7), take(7), take(7)
    low_sems, high_sems = take(6), take(6)
    scratch = refs
    ring = Ring(dims)
    count, width = secs[0] * secs[1], secs[1]
    me = lax.axis_index("section")
    y0, x0 = me // width, lax.rem(me, width)
    peers = [{"section": lax.rem(me + j, count)} for j in range(1, count)]
    across = {"section": (1 - y0) * width + x0}
    beside = [{"section": y0 * width + lax.rem(x0 + j, width)} for j in range(1, width)]
    down, up, back = swap_down(dims, count), swap_up(dims, count), swap_down(dims, count)
    gather = Fan(ring, count, gb_ref, ring_part)
    entry = Entry(ring.peers + peers, (down, up, gather))
    entry.count = entry.count + dims[0] - 1 + len(gather.far)
    loads = [pltpu.make_async_copy(e_hbm, e_ref, load_e), pltpu.make_async_copy(c_hbm, c_ref, load_c)]
    for load in loads:
        load.start()
    work = make(sec_ref, col_ref, e_ref, c_ref, wide_ref, et_ref, ct_ref, e2_ref)

    rows, rank = a_ref.shape
    high = b_rows.shape[0]
    half = rows // 2
    value = (a_ref[...].astype(F32) * gain_ref[...]).astype(BF)
    scaled[...] = value
    turned = lax.dot_general(eye(high, half), b_ref[...], NT, preferred_element_type=F32)
    b_rows[...] = turned.astype(BF)
    value = value.astype(F32)
    upper = ring.y < dims[0] // 2
    rest = jnp.where(upper, value[half:], value[:half])
    if high > half:
        rest = jnp.concatenate([rest, jnp.zeros((high - half, rank), F32)], axis=0)
    give[...] = rest.astype(BF)
    entry.wait()
    exchange = remote(give, other, hsend, hrecv, ring.rows[dims[0] // 2 - 1])
    exchange.start()
    down.start(scaled, own_col.at[pl.ds(0, rows)], asems)
    up.start(b_rows, own_col.at[pl.ds(rows, high)], bsems)
    for load in loads:
        load.wait()
    work.tokens()
    exchange.wait_recv()
    both = jnp.where(upper, value[:half], value[half:]) + other[...].astype(F32)[:half]
    own_sec[...] = jnp.concatenate([both, turned[:half]], axis=0).astype(BF)
    first = Spread(ring, own_sec, sec_ref, first_sems)
    second = Spread(ring, own_col, col_ref, second_sems)
    third = Spread(ring, total_ref, gall_ref, third_sems)
    last = dims[1] // 2
    sent = []

    def push(*what):
        copy = remote(*what)
        copy.start()
        sent.append(copy)

    first.start()
    first.first()
    down.wait()
    up.wait()
    second.start()
    first.step(1)
    second.first()
    for k in range(1, last + 1):
        second.step(k)
        if k < last:
            first.step(k + 1)
    second.landed()
    work.gram(gram_ref)
    for j in range(1, count):
        push(gram_ref, landing.at[me], gsend.at[j], grecv.at[j], peers[j - 1])
    landing[me] = gram_ref[...]
    first.landed()
    work.project(proj_ref)
    own = pltpu.make_async_copy(proj_ref, pall_ref.at[y0, x0], local_sem)
    own.start()
    push(proj_ref, pall_ref.at[y0, x0], across_send, across_recv, across)
    for j in range(1, width):
        push(proj_ref, pall_ref.at[y0, x0], xsend.at[0, j], xrecv.at[0, j], beside[j - 1])
    for j in range(1, count):
        block = landing.at[lax.rem(me + count - j, count)]
        remote(block, block, gsend.at[j], grecv.at[j], peers[j - 1]).wait_recv()
    total = landing[0].astype(F32)
    for i in range(1, count):
        total = total + landing[i].astype(F32)
    total_ref[...] = total.astype(BF)
    third.start()
    third.first()
    third.step(1)
    block = pall_ref.at[1 - y0, x0]
    remote(block, block, across_send, across_recv, across).wait_recv()
    for j in range(1, width):
        push(block, block, xsend.at[1, j], xrecv.at[1, j], beside[j - 1])
    for k in range(2, last + 1):
        third.step(k)
    for h in range(2):
        for j in range(1, width):
            landed = pall_ref.at[y0 if h == 0 else 1 - y0, lax.rem(x0 + width - j, width)]
            remote(landed, landed, xsend.at[h, j], xrecv.at[h, j], beside[j - 1]).wait_recv()
    third.landed()
    own.wait()
    given = (pall_ref, e2_ref, gall_ref, et_ref, ct_ref, col_ref)
    raised = Scatter(ring, x_ref, pl.ds(rows, high), high_buffers, high_sems)
    lower = Scatter(ring, x_ref, pl.ds(0, rows), low_buffers, low_sems)
    solver = compute(given, x_ref, ge_ref, scratch)
    solver.ups()
    raised.start()
    raised.step(0)
    solver.downs()
    lower.start()
    last = dims[1] // 2
    for k in range(1, last + 1):
        raised.step(k)
        if k > 1 or last == 1:
            lower.step(max(k - 2, 0))
    raised.rows_start()
    if last > 1:
        lower.step(last - 1)
    mine_high[...] = raised.rows_finish().astype(BF)
    gather.start_from(mine_high)
    lower.step(last)
    lower.rows_start()
    solver.rest()
    mine_low[...] = lower.rows_finish().astype(BF)
    back.start(mine_low, got_low, csems)
    gather.first()
    back.wait()
    w = got_low[...].astype(F32)
    ga_ref[...] = w * gain_ref[...]
    prod = w * a_ref[...].astype(F32)
    if rank > rows:
        prod = jnp.concatenate([prod, jnp.zeros((rank - rows, rank), F32)], axis=0)
    line = lax.dot_general(
        jnp.ones((8, rank), F32), prod, NT, precision=lax.Precision.HIGHEST, preferred_element_type=F32
    )
    gg_ref[me] = line.astype(BF).astype(F32)
    for j in range(1, count):
        copy = remote(gg_ref.at[me], gg_ref.at[me], tsend.at[j], trecv.at[j], peers[j - 1])
        copy.start()
        sent.append(copy)
    gather.collect()
    gather.landed()
    for y in range(dims[0]):
        pieces = [gb_ref[y, z, c].astype(F32)[:half] for z in range(dims[1]) for c in range(dims[2])]
        piece = jnp.concatenate(pieces, axis=0).astype(BF)
        span = piece.shape[0]
        up_ref[:, y * span : (y + 1) * span] = dot_nt(eye(rank, rank), piece)
    for j in range(1, count):
        block = gg_ref.at[lax.rem(me + count - j, count)]
        remote(block, block, tsend.at[j], trecv.at[j], peers[j - 1]).wait_recv()
    for parity in range(2):
        total = gg_ref[parity]
        for i in range(parity + 2, count, 2):
            total = total + gg_ref[i]
        gain_out[parity : parity + 1] = total[:1, :rows]
    gather.drain()
    for copy in sent:
        copy.wait_send()
    raised.finish()
    lower.finish()
    first.drain()
    second.drain()
    third.drain()
    exchange.wait_send()


def whole(a, b, gain, embeds, cotangent, make, compute, scratch, dims=DP, secs=SEC, high=64):
    rows, rank = a.shape
    count = secs[0] * secs[1]
    tokens, width = embeds.shape
    cols = width // count
    dma = pltpu.SemaphoreType.DMA
    vmem = pl.BlockSpec(memory_space=pltpu.VMEM)
    anywhere = pl.BlockSpec(memory_space=pl.ANY)
    tall = rows + high
    shape = jax.ShapeDtypeStruct

    def buffer(*size, kind=BF):
        return pltpu.VMEM(size, kind)

    return pl.pallas_call(
        functools.partial(whole_kernel, dims, secs, make, compute),
        out_shape=[
            shape(a.shape, F32),
            shape((rank, width), F32),
            shape((2, rows), F32),
            shape((tokens, cols), BF),
        ],
        in_specs=[vmem] * 3 + [anywhere] * 2,
        out_specs=[vmem] * 4,
        scratch_shapes=[buffer(n, rank) for n in (rows, high, high, high, rows, tall)]
        + [
            buffer(*dims, rows, rank),
            buffer(*dims, tall, rank),
            buffer(tokens, width),
            buffer(tokens, width),
            buffer(width, 2 * rank),
            buffer(tokens, 3 * rank),
            buffer(rank, rank),
            buffer(count, rank, rank),
            buffer(rank, rank),
            buffer(*dims, rank, rank),
            buffer(*secs, tokens, 3 * rank),
            buffer(cols, tokens),
            buffer(cols, tokens),
            buffer(tokens, 128, kind=F32),
            buffer(*dims, high, rank),
            buffer(count, 8, rank, kind=F32),
            buffer(*dims, tall, rank),
        ]
        + [buffer(n, rank) for n in (rows, rows, high)]
        + scatter_buffers(dims, rows, rank)
        + scatter_buffers(dims, high, rank)
        + [dma] * 4
        + [dma((3,))] * 3
        + [dma((count,))] * 4
        + [dma] * 3
        + [dma((2, secs[1]))] * 2
        + ring_sems(dims) * 4
        + scatter_sems(dims) * 2
        + scratch,
        compiler_params=pltpu.CompilerParams(
            collective_id=0, has_side_effects=True, vmem_limit_bytes=58 * 2**20
        ),
    )(a, b, gain, embeds, cotangent)


def dp_spot(index):
    return index // 16, index // 2 % 8, index % 2


class Solver:
    def __init__(self, given, x_ref, ge_ref, scratch):
        self.given, self.x, self.ge = given, x_ref, ge_ref
        self.r, self.v, self.w, self.hb, self.h, self.acc = scratch
        self.col = given[5]

    def down_rows(self, half, t):
        quarter = self.h.shape[1] // 4
        first = half * 4 * CALLS + t * 4
        return jnp.concatenate([self.col[dp_spot(first + j)][:quarter] for j in range(4)], axis=0)

    def up_rows(self, t):
        quarter = self.h.shape[1] // 4
        eighth = quarter // 2
        pieces = [self.col[dp_spot(t * 8 + j)][quarter:].astype(F32)[:eighth] for j in range(8)]
        return jnp.concatenate(pieces, axis=0).astype(BF)

    def put(self, index, rows, value):
        self.x[(*dp_spot(index), rows)] = value

    def ups(self):
        proj_ref, e2_ref, gram_ref, et_ref, ct_ref, _ = self.given
        r_ref, v_ref, w_ref, hb_ref, h_ref, acc_ref = self.r, self.v, self.w, self.hb, self.h, self.acc
        tokens, rank = r_ref.shape[1:]
        cols = et_ref.shape[0]
        scale = 1.0 / (2 * cols * CALLS)

        def gram(t, pos):
            return gram_ref[dp_spot(14 * t + pos if 2 * t < CALLS else 16 * (CALLS - 1 - t) + pos + 1)]

        e2 = e2_ref[:, :1]
        h2 = e2
        invs = []
        for s in range(CALLS):
            pre = proj_ref[s // 4, s % 4, :, :rank].astype(F32)
            hb = proj_ref[s // 4, s % 4, :, rank : 2 * rank].astype(F32)
            for t in range(s):
                pre = pre + dot(r_ref[t], gram(t, 2 * s - 1))
                hb = hb + dot(r_ref[t], gram(t, 2 * s))
            inv = lax.rsqrt((e2 + h2) * scale + EPS)
            invs.append(inv)
            r = (pre * inv).astype(BF)
            r_ref[s] = r
            rn = dot(r, gram(s, 2 * s))
            h2 = h2 + jnp.sum(r.astype(F32) * (2.0 * hb + rn), axis=1, keepdims=True)
            hb_ref[s] = hb + rn

        lane = lax.broadcasted_iota(jnp.int32, (tokens, rank), 1)
        kap = jnp.zeros((tokens, 1), F32)
        kmat = jnp.zeros((tokens, rank), F32)
        for s in reversed(range(CALLS)):
            u = proj_ref[s // 4, s % 4, :, 2 * rank :].astype(F32) - kap * hb_ref[s]
            for t in range(s + 1, CALLS):
                u = u + dot_nt(v_ref[t], gram(s, 2 * t - 1)) + dot_nt(w_ref[t], gram(s, 2 * t))
            u = u.astype(BF).astype(F32)
            r = r_ref[s].astype(F32)
            inv = invs[s]
            q = jnp.sum(u * r, axis=1, keepdims=True) * scale
            k = inv * inv * q
            v_ref[s] = (inv * u).astype(BF)
            w_ref[s] = (-kap * r).astype(BF)
            kmat = jnp.where(lane == s, k, kmat)
            kap = kap + k

        unit = (
            lax.broadcasted_iota(jnp.int32, (CALLS, rank), 0) == lax.broadcasted_iota(jnp.int32, (CALLS, rank), 1)
        ).astype(F32)
        krows = lax.dot_general(unit, kmat, NT, precision=lax.Precision.HIGHEST, preferred_element_type=F32)

        quarter, eighth = cols // 4, cols // 8
        filler = jnp.zeros((64 - eighth, rank), F32)
        h_ref[0] = et_ref[...]
        for t in range(CALLS - 1):
            h_ref[t + 1] = (h_ref[t].astype(F32) + dot_nt(self.up_rows(t), r_ref[t])).astype(BF)
        back = ct_ref[...]
        for t in reversed(range(CALLS)):
            part = dot(back, r_ref[t])
            for j in range(8):
                piece = jnp.concatenate([part[j * eighth : (j + 1) * eighth], filler], axis=0)
                self.put(t * 8 + j, pl.ds(quarter, 64), piece.astype(BF))
            step = dot_nt(self.down_rows(0, t), v_ref[t]) - krows[t : t + 1] * h_ref[t].astype(F32)
            back = (back.astype(F32) + step).astype(BF)
        total = back.astype(F32) - jnp.sum(krows, axis=0, keepdims=True) * et_ref[...].astype(F32)
        acc_ref[...] = total

    def downs(self):
        et_ref = self.given[3]
        quarter = self.h.shape[1] // 4
        for t in range(CALLS):
            for half, source in ((0, self.h[t]), (1, et_ref[...])):
                value = dot(source, self.v[t]).astype(BF)
                for j in range(4):
                    index = half * 4 * CALLS + t * 4 + j
                    self.put(index, pl.ds(0, quarter), value[j * quarter : (j + 1) * quarter])

    def rest(self):
        for t in range(CALLS):
            self.acc[...] += dot_nt(self.down_rows(1, t), self.v[t])
        cols = self.acc.shape[0]
        turned = lax.dot_general(
            self.acc[...].astype(BF), eye(cols, cols), (((0,), (0,)), ((), ())), preferred_element_type=F32
        )
        self.ge[...] = turned.astype(BF)


def per_device(embeds, cotangent, adapter_a, adapter_b, norm_gains):
    sec, dp = lax.axis_index("section"), lax.axis_index("dp")
    tokens, width = embeds.shape
    cols = width // CALLS
    a_own = adapter_a[0]
    quarter, rank = a_own.shape
    eighth = quarter // 2
    gain = jnp.where(sec % 2 == 0, norm_gains[0], norm_gains[1])
    gain_rows = lax.dynamic_slice_in_dim(gain, dp * quarter, quarter, 0)
    gain_rows = jnp.broadcast_to(gain_rows[:, None], (quarter, rank))
    scratch = [
        pltpu.VMEM((CALLS, tokens, rank), BF),
        pltpu.VMEM((CALLS, tokens, rank), BF),
        pltpu.VMEM((CALLS, tokens, rank), BF),
        pltpu.VMEM((CALLS, tokens, rank), F32),
        pltpu.VMEM((CALLS, cols, tokens), BF),
        pltpu.VMEM((cols, tokens), F32),
    ]
    grad_a, grad_b, grad_gain, grad_embed = whole(
        a_own, adapter_b[0], gain_rows, embeds, cotangent, Front, Solver, scratch
    )
    return (grad_a[None], grad_b[None], grad_gain, grad_embed)


def solution(mesh):
    in_specs = (
        P("dp", None),
        P("dp", None),
        P("section", "dp", None),
        P("section", None, "dp"),
        P(),
    )
    out_specs = (
        P("section", "dp", None),
        P("section", None, None),
        P(None, "dp"),
        P("dp", "section"),
    )
    return jax.shard_map(per_device, mesh=mesh, in_specs=in_specs, out_specs=out_specs, check_vma=False)
```
